1024 devices in a mesh: rows: 64 (over y, x), cols: 16 (over z, core).
Axes of the slice: x: 8, y: 8, z: 8, core: 2. Of those that a mesh axis runs over, the one named last changes fastest.
Arguments:
- head_start: float32 [8, 2048, 2048], P(None, 'rows', 'cols'), may hold values from -6 to 6
- class_map: int32 [8, 2048, 2048], P(None, 'rows', 'cols'), may hold values from 0 to 7
- class_cond: float32 [8], replicated, may hold values from 1 to 10
- partials: float32 [64, 16, 16, 32, 128], P('rows', 'cols'), may hold values from -6 to 6
- send_count: int32 [64, 16, 16], P('rows', 'cols'), may hold values from 1 to 32, as said below
- recv_block: int32 [64, 16, 16, 32], P('rows', 'cols'), may hold values from 0 to 255
Outputs:
- head: float32 [8, 2048, 2048], P(None, 'rows', 'cols')
- residual: float32 [8, 2048, 2048], P(None, 'rows', 'cols')
The draws below stay inside these ranges and needn't reach their ends.
Inputs may be any that keep to these rules, and one draw needn't show every extreme that they name: `send_count`: live slots of one sender to one receiver; in each row group some sender fills all 32 slots to one receiver and sends a single one to another. `recv_block`: blocks are numbered z * 32 + local y.
All inputs are finite; a program needn't handle non-finite values.
Results may differ from the reference program's by a relative error of at most 0.00013.
Values sent between devices are 32-bit elements; how exact they have to be, the bound alone decides.
No kernel may reach another device: no remote copies, remote signals or barrier semaphores. Data moves between devices by JAX's collectives and lax.ppermute only.
A program may use at most 32 MiB of HBM per device.

```python
import math
import jax
import jax.numpy as jnp
from jax import lax

CX = 128
CY = 32
SLOTS = 32
NZ = 8
NCLASS = 8
NU1 = 2
NU2 = 2
NUC = 4
NX = 2048
NY = 2048
N_ROWS = 64
N_COLS = 16


def draw_send_count(key, part):
    first, second = jax.random.split(jax.random.fold_in(key, 17))
    shape = (N_ROWS, N_COLS, N_COLS)
    counts = jax.random.randint(first, shape, 1, SLOTS + 1)
    offset = jax.random.randint(second, (N_ROWS, 1, 1), 0, N_COLS)
    source = lax.broadcasted_iota(jnp.int32, shape, 1)
    target = lax.broadcasted_iota(jnp.int32, shape, 2)
    single = target == (source + offset + 1) % N_COLS
    full = target == (source + offset) % N_COLS
    counts = jnp.where(single, 1, counts)
    counts = jnp.where(full, SLOTS, counts)
    return counts.astype(jnp.int32)


def with_ends(drawn, key, smallest, top_value):
    spot = [jax.random.randint(jax.random.fold_in(key, axis), (), 0, length) for axis, length in enumerate(drawn.shape)]
    longest = drawn.shape.index(max(drawn.shape))
    next_to = spot[:longest] + [(spot[longest] + 1) % drawn.shape[longest]] + spot[longest + 1:]
    return drawn.at[tuple(spot)].set(smallest).at[tuple(next_to)].set(top_value)


def block_scale(own_key, extent, pieces, smallest, largest):
    loudness, own = 1.0, jax.random.fold_in(own_key, 6)
    for dim, parts in pieces:
        steps = jnp.exp(jax.random.uniform(jax.random.fold_in(own, dim), (parts,), jnp.float32, smallest / len(pieces), largest / len(pieces)))
        loudness = loudness * jnp.repeat(steps, extent[dim] // parts).reshape([-1 if axis == dim else 1 for axis in range(len(extent))])
    return loudness


def gaussian(key, shape, scale, bound, pieces=(), kind=jnp.bfloat16):
    entries = scale * jax.random.normal(key, shape, jnp.float32)
    if pieces:
        entries = entries * block_scale(key, shape, pieces, -0.22, 0.18)
    return jnp.clip(entries, -bound, bound).astype(kind)


def setup_inputs(seed: int = 0) -> dict:
    seeds = jax.random.split(jax.random.key(seed), 7)
    head_start = gaussian(seeds[0], (NZ, NY, NX), 1.0, 6.0, ((1, 64), (2, 16)), jnp.float32)
    class_map = with_ends(jax.random.randint(seeds[1], (NZ, NY, NX), 0, NCLASS), jax.random.fold_in(seeds[1], 1), 0, NCLASS - 1).astype(jnp.int32)
    class_cond = jnp.clip(jnp.exp(jax.random.uniform(seeds[2], (NCLASS,), jnp.float32, math.log(1.0), math.log(10.0))), 1.0, 10.0)
    partials = gaussian(seeds[3], (N_ROWS, N_COLS, N_COLS, SLOTS, CX), 1.0, 6.0, ((0, 64), (1, 16)), jnp.float32)
    send_count = draw_send_count(jax.random.fold_in(seeds[6], 71), 0)
    recv_block = with_ends(jax.random.randint(seeds[5], (N_ROWS, N_COLS, N_COLS, SLOTS), 0, NZ * CY), jax.random.fold_in(seeds[5], 1), 0, (NZ * CY) - 1).astype(jnp.int32)
    return {"head_start": head_start, "class_map": class_map, "class_cond": class_cond, "partials": partials, "send_count": send_count, "recv_block": recv_block}


OMEGA = 0.8


def pad_plane(field):
    return jnp.pad(field, ((0, 0), (1, 1), (1, 1)))


def diagonal_of(cond_pad, zweight):
    center = cond_pad[:, 1:-1, 1:-1]
    total = jnp.zeros_like(center)
    for ylo, xlo in ((0, 1), (2, 1), (1, 0), (1, 2)):
        neighbour = cond_pad[:, ylo:ylo + center.shape[1], xlo:xlo + center.shape[2]]
        total = total + 0.5 * (center + neighbour)
    vertical = zweight * 0.5 * (center[1:] + center[:-1])
    total = total + jnp.pad(vertical, ((0, 1), (0, 0), (0, 0))) + jnp.pad(vertical, ((1, 0), (0, 0), (0, 0)))
    return total


def apply_op(field_pad, cond_pad, zweight):
    center = cond_pad[:, 1:-1, 1:-1]
    value = field_pad[:, 1:-1, 1:-1]
    total = jnp.zeros_like(value)
    for ylo, xlo in ((0, 1), (2, 1), (1, 0), (1, 2)):
        neighbour = cond_pad[:, ylo:ylo + center.shape[1], xlo:xlo + center.shape[2]]
        other = field_pad[:, ylo:ylo + center.shape[1], xlo:xlo + center.shape[2]]
        total = total + 0.5 * (center + neighbour) * (value - other)
    vertical = zweight * 0.5 * (center[1:] + center[:-1]) * (value[1:] - value[:-1])
    total = total + jnp.pad(vertical, ((0, 1), (0, 0), (0, 0))) - jnp.pad(vertical, ((1, 0), (0, 0), (0, 0)))
    return total


def restrict_sum(field):
    depth, height, width = field.shape
    return jnp.sum(field.reshape(depth, height // 2, 2, width // 2, 2), axis=(2, 4))


def reference(head_start, class_map, class_cond, partials, send_count, recv_block):
    cond = class_cond[class_map]
    groups, ncols = partials.shape[0], partials.shape[1]
    slots, width = partials.shape[3], partials.shape[4]
    depth, height = head_start.shape[0], head_start.shape[1] // groups
    blocks = depth * height
    live = lax.broadcasted_iota(jnp.int32, send_count.shape + (slots,), 3) < send_count[..., None]
    masked = partials * live[..., None].astype(jnp.float32)
    block_ids = jnp.transpose(recv_block, (0, 2, 1, 3)).astype(jnp.int32)
    group_ids = lax.broadcasted_iota(jnp.int32, block_ids.shape, 0)
    target_ids = lax.broadcasted_iota(jnp.int32, block_ids.shape, 2)
    segment = (group_ids * ncols + target_ids) * blocks + block_ids
    summed = jax.ops.segment_sum(masked.reshape(-1, width), segment.reshape(-1), num_segments=groups * ncols * blocks)
    summed = summed.reshape(groups, ncols, depth, height, width)
    recharge = jnp.transpose(summed, (2, 0, 3, 1, 4)).reshape(head_start.shape)

    cond_pad = pad_plane(cond)
    fine_diag = diagonal_of(cond_pad, 1.0)
    head = head_start
    for sweep in range(NU1):
        head = head + OMEGA * (recharge - apply_op(pad_plane(head), cond_pad, 1.0)) / fine_diag
    fine_res = recharge - apply_op(pad_plane(head), cond_pad, 1.0)
    coarse_src = restrict_sum(fine_res)
    coarse_cond = 0.25 * restrict_sum(cond)
    coarse_pad = pad_plane(coarse_cond)
    coarse_diag = diagonal_of(coarse_pad, 4.0)
    correction = OMEGA * coarse_src / coarse_diag
    for sweep in range(NUC - 1):
        correction = correction + OMEGA * (coarse_src - apply_op(pad_plane(correction), coarse_pad, 4.0)) / coarse_diag
    head = head + jnp.repeat(jnp.repeat(correction, 2, axis=1), 2, axis=2)
    for sweep in range(NU2):
        head = head + OMEGA * (recharge - apply_op(pad_plane(head), cond_pad, 1.0)) / fine_diag
    residual = recharge - apply_op(pad_plane(head), cond_pad, 1.0)
    return head, residual
```

```python
import jax
import jax.numpy as jnp
from jax import lax
from jax.experimental import pallas as pl
from jax.experimental.pallas import tpu as pltpu
from jax.sharding import PartitionSpec as P

NZ, CY, CX, SLOTS = 8, 32, 128, 32
OMEGA = 0.8
NU1, NU2, NUC = 2, 2, 4
HY, HX = 14, 16
RY = 12
ROWS = CY + 2 * HY
LANES = 2 * CX
F32 = jnp.float32


def lane_of(shape):
    return lax.broadcasted_iota(jnp.int32, shape, len(shape) - 1)


def packed(rows, lane):
    out = None
    for q, row in enumerate(rows):
        turned = pltpu.roll(row, 32 * q + 16, 1)
        out = turned if q == 0 else jnp.where(lane // 32 == q, turned, out)
    return out


def unpacked(block, q, lane):
    turned = pltpu.roll(block, (CX - 32 * q - 16) % CX, 1)
    return jnp.where((lane < HX) | (lane >= CX - HX), turned, 0.0)


def outgoing_kernel(count_ref, partials_ref, out_ref):
    ncols = partials_ref.shape[0]
    lane = lane_of((8, CX))
    slot = lax.broadcasted_iota(jnp.int32, (8, CX), 0)
    strips = []
    for d in range(ncols):
        rows = []
        for q in range(SLOTS // 8):
            row = jnp.where(slot + 8 * q < count_ref[d], partials_ref[d, 8 * q : 8 * q + 8, :], 0.0)
            out_ref[d, 8 * q : 8 * q + 8, :] = row
            rows.append(row)
        strips.append(packed(rows, lane))
    zero = jnp.zeros((8, CX), F32)
    for d in range(ncols):
        left = strips[d - 1] if d > 0 else zero
        right = strips[d + 1] if d < ncols - 1 else zero
        out_ref[d, SLOTS : SLOTS + 8, :] = jnp.where(lane % 32 < HX, left, right)


def fields_kernel(class_cond_ref, head_ref, class_ref, ids_ref, head_out, cond_out, strip_out):
    lane = lane_of((8, CX))
    values = [class_cond_ref[c] for c in range(8)]
    for block in range(CY // 4):
        heads, conds = [], []
        for q in range(4):
            y = 4 * block + q
            head = head_ref[pl.ds(y, NZ, stride=CY), :]
            kind = class_ref[pl.ds(y, NZ, stride=CY), :]
            cond = jnp.full((8, CX), values[0], F32)
            for c in range(1, 8):
                cond = jnp.where(kind == c, values[c], cond)
            head_out[y] = head
            cond_out[y] = cond
            heads.append(head)
            conds.append(cond)
        strip_out[block] = packed(heads, lane)
        strip_out[CY // 4 + block] = packed(conds, lane)
    strip_out[CY // 2] = ids_ref[...]


def recharge_kernel(incoming_ref, ids_ref, left_ref, right_ref, head_ref, cond_ref, main_out, halo_out, up_out, down_out):
    ncols = incoming_ref.shape[0]
    total = ncols * SLOTS
    chunk = min(256, total)
    senders = chunk // SLOTS
    lane = lane_of((8, CX))
    row = lax.broadcasted_iota(jnp.int32, (NZ * CY, chunk), 0)
    block_of = ((row % NZ) * CY + row // NZ).astype(F32)

    def onehot(ids, m):
        flat = jnp.concatenate([ids[r : r + 1, :] for r in range(m * chunk // CX, (m + 1) * chunk // CX)], axis=1)
        return jnp.where(block_of == flat, 1.0, 0.0).astype(jnp.bfloat16)

    def halves(values):
        high = values.astype(jnp.bfloat16)
        low = (values - high.astype(F32)).astype(jnp.bfloat16)
        return jnp.concatenate([high, low], axis=1)

    own, left, right = ids_ref[...], left_ref[CY // 2], right_ref[CY // 2]
    main = jnp.zeros((NZ * CY, LANES), F32)
    from_left = jnp.zeros((NZ * CY, LANES), F32)
    from_right = jnp.zeros((NZ * CY, LANES), F32)
    for m in range(total // chunk):
        values = incoming_ref[m * senders : (m + 1) * senders, 0:SLOTS, :].reshape(chunk, CX)
        main = main + jnp.dot(onehot(own, m), halves(values), preferred_element_type=F32)
        strips = []
        for s in range(m * senders, (m + 1) * senders):
            strip = incoming_ref[s, SLOTS : SLOTS + 8, :]
            strips += [pltpu.roll(strip, (CX - 32 * q - 16) % CX, 1) for q in range(4)]
        edges = halves(jnp.concatenate(strips, axis=0))
        from_left = from_left + jnp.dot(onehot(left, m), edges, preferred_element_type=F32)
        from_right = from_right + jnp.dot(onehot(right, m), edges, preferred_element_type=F32)
    main = (main[:, :CX] + main[:, CX:]).reshape(CY, NZ, CX)
    from_left = (from_left[:, :CX] + from_left[:, CX:]).reshape(CY, NZ, CX)
    from_right = (from_right[:, :CX] + from_right[:, CX:]).reshape(CY, NZ, CX)
    wide = lane_of((CY, NZ, CX))
    halo = jnp.where(wide >= CX - HX, from_left, jnp.where(wide < HX, from_right, 0.0))
    main_out[...] = main
    halo_out[...] = halo
    for out, first, strip0 in ((up_out, 0, 0), (down_out, CY - HY, CY // 4 - 4)):
        skip = first and HY - RY
        out[0:HY] = head_ref[first : first + HY]
        out[HY : 2 * HY] = cond_ref[first : first + HY]
        out[2 * HY : 2 * HY + RY] = main[first + skip : first + skip + RY]
        base = 2 * HY + RY
        for i in range(4):
            for f in range(2):
                at = f * (CY // 4) + strip0 + i
                out[base + 4 * f + i] = jnp.where(lane % 32 < HX, left_ref[at], right_ref[at])
        for i in range(RY // 4):
            y = first + skip + 4 * i
            out[base + 8 + i] = packed([halo[y + q] for q in range(4)], lane)


SENT = 2 * HY + RY + 8 + RY // 4


def cycle_kernel(place_ref, head_ref, cond_ref, main_ref, halo_ref, left_ref, right_ref, top_ref, bottom_ref,
                 head_out, residual_out,
                 u0, u1, cond, source, face_x, face_y, face_z, weight,
                 c_cond, c_src, c_u0, c_u1, c_x, c_y, c_z, c_weight):
    lane = lane_of((8, CX))
    for y in range(CY):
        r = HY + y
        u0[r, :, 0:CX] = head_ref[y]
        cond[r, :, 0:CX] = cond_ref[y]
        source[r, :, 0:CX] = main_ref[y]
        source[r, :, CX:LANES] = halo_ref[y]
    for i in range(CY // 4):
        for f, field in ((0, u0), (1, cond)):
            at = f * (CY // 4) + i
            block = jnp.where(lane % 32 < HX, left_ref[at], right_ref[at])
            for q in range(4):
                field[HY + 4 * i + q, :, CX:LANES] = unpacked(block, q, lane)
    base = 2 * HY + RY
    for ref, row0, shift, rrow, in ((top_ref, 0, 2, HY - RY), (bottom_ref, HY + CY, 0, HY + CY)):
        for i in range(HY):
            for f, field in ((0, u0), (1, cond)):
                field[row0 + i, :, 0:CX] = ref[f * HY + i]
                field[row0 + i, :, CX:LANES] = unpacked(ref[base + 4 * f + (i + shift) // 4], (i + shift) % 4, lane)
        for i in range(RY):
            source[rrow + i, :, 0:CX] = ref[2 * HY + i]
            source[rrow + i, :, CX:LANES] = unpacked(ref[base + 8 + i // 4], i % 4, lane)

    g, d, ngroups, ncols = place_ref[0], place_ref[1], place_ref[2], place_ref[3]

    def over_rows(first, last, step, body):
        count = last - first + 1
        assert count % step == 0
        pl.loop(0, count // step)(lambda i: body(first + i * step))

    def turn(x, by):
        return pltpu.roll(x, by % LANES, x.ndim - 1)

    def turn_z(x, by):
        return pltpu.roll(x, by % NZ, x.ndim - 2)

    def inside(shape, r, factor):
        at = lane_of(shape)
        x = jnp.where(at < CX + HX, at, jnp.where(at >= LANES - HX, at - LANES, -(1 << 20))) + d * CX
        y = lax.broadcasted_iota(jnp.int32, shape, 0) + (r - HY // factor) + g * (CY // factor)
        return (x >= 0) & (x < ncols * CX) & (y >= 0) & (y < ngroups * (CY // factor))

    def faces(k, fx, fy, fz, shift, zweight, first, last, step):
        def body(r):
            c = k[pl.ds(r, step + 1)]
            low, high = c[:-1], c[1:]
            fx[pl.ds(r, step)] = 0.5 * (low + turn(low, -shift))
            fy[pl.ds(r, step)] = 0.5 * (low + high)
            z = lax.broadcasted_iota(jnp.int32, low.shape, 1)
            fz[pl.ds(r, step)] = jnp.where(z < NZ - 1, (0.5 * zweight) * (low + turn_z(low, -1)), 0.0)

        over_rows(first, last, step, body)

    def weights(fx, fy, fz, w, shift, factor, first, last, step):
        def body(r):
            x, z = fx[pl.ds(r, step)], fz[pl.ds(r, step)]
            y = fy[pl.ds(r - 1, step + 1)]
            total = x + turn(x, shift) + y[1:] + y[:-1] + z + turn_z(z, 1)
            ok = inside(total.shape, r, factor)
            w[pl.ds(r, step)] = jnp.where(ok, OMEGA / jnp.where(ok, total, 1.0), 0.0)

        over_rows(first, last, step, body)

    def operator(u, fx, fy, fz, shift, r, step):
        v = u[pl.ds(r - 1, step + 2)]
        own = v[1:-1]
        x = fx[pl.ds(r, step)] * (own - turn(own, -shift))
        y = fy[pl.ds(r - 1, step + 1)] * (v[:-1] - v[1:])
        z = fz[pl.ds(r, step)] * (turn_z(own, -1) - own)
        return own, (x - turn(x, shift)) + (y[1:] - y[:-1]) + (z - turn_z(z, 1))

    def sweep(old, new, src, fx, fy, fz, w, shift, first, last, step):
        def body(r):
            own, applied = operator(old, fx, fy, fz, shift, r, step)
            new[pl.ds(r, step)] = own + w[pl.ds(r, step)] * (src[pl.ds(r, step)] - applied)

        over_rows(first, last, step, body)

    def pairs(x):
        even = lane_of(x.shape) % 2 == 0
        return x + jnp.where(even, turn(x, -1), turn(x, 1))

    fine = (face_x, face_y, face_z)
    coarse = (c_x, c_y, c_z)
    faces(cond, *fine, 1, 1.0, 0, ROWS - 3, 2)
    faces(cond, *fine, 1, 1.0, ROWS - 2, ROWS - 2, 1)
    weights(*fine, weight, 1, 1, 2, ROWS - 3, 2)
    sweep(u0, u1, source, *fine, weight, 1, 2, ROWS - 3, 2)
    sweep(u1, u0, source, *fine, weight, 1, 3, ROWS - 4, 2)

    def restrict_cond(c):
        k = cond[pl.ds(2 * c, 2)]
        c_cond[pl.ds(c, 1)] = 0.25 * pairs(k[0:1] + k[1:2])

    over_rows(0, ROWS // 2 - 1, 1, restrict_cond)
    faces(c_cond, *coarse, 2, 4.0, 0, ROWS // 2 - 3, 2)
    weights(*coarse, c_weight, 2, 2, 2, ROWS // 2 - 3, 2)

    def restrict_residual(c):
        r = 2 * c
        _, applied = operator(u0, *fine, 1, r, 2)
        res = source[pl.ds(r, 2)] - applied
        summed = pairs(res[0:1] + res[1:2])
        c_src[pl.ds(c, 1)] = summed
        c_u0[pl.ds(c, 1)] = c_weight[pl.ds(c, 1)] * summed

    over_rows(2, ROWS // 2 - 3, 1, restrict_residual)
    old, new = c_u0, c_u1
    for i in range(1, NUC):
        sweep(old, new, c_src, *coarse, c_weight, 2, 2 + i, ROWS // 2 - 3 - i, 2)
        old, new = new, old

    def prolong(c):
        u0[pl.ds(2 * c, 2)] = u0[pl.ds(2 * c, 2)] + old[pl.ds(c, 1)]

    over_rows(5, ROWS // 2 - 6, 1, prolong)
    sweep(u0, u1, source, *fine, weight, 1, 12, ROWS - 13, 2)
    sweep(u1, u0, source, *fine, weight, 1, 13, ROWS - 14, 2)

    def finish(r):
        own, applied = operator(u0, *fine, 1, r, 2)
        res = source[pl.ds(r, 2)] - applied
        for i in range(2):
            head_out[pl.ds(r + i - HY, NZ, stride=CY), :] = own[i, :, 0:CX]
            residual_out[pl.ds(r + i - HY, NZ, stride=CY), :] = res[i, :, 0:CX]

    over_rows(HY, HY + CY - 1, 2, finish)


VMEM = pl.BlockSpec(memory_space=pltpu.VMEM)
SMEM = pl.BlockSpec(memory_space=pltpu.SMEM)


def call(kernel, ins, outs, scratch=(), flops=1 << 20, nbytes=1 << 20):
    return pl.pallas_call(
        kernel,
        out_shape=tuple(jax.ShapeDtypeStruct(s, F32) for s in outs),
        in_specs=[SMEM if i else VMEM for i in ins],
        out_specs=tuple(VMEM for _ in outs),
        scratch_shapes=[pltpu.VMEM(s, F32) for s in scratch],
        cost_estimate=pl.CostEstimate(flops=flops, bytes_accessed=nbytes, transcendentals=0),
        compiler_params=pltpu.CompilerParams(vmem_limit_bytes=32 << 20),
    )


def forward(count):
    return [(i, i + 1) for i in range(count - 1)]


def backward(count):
    return [(i + 1, i) for i in range(count - 1)]


def body(head_start, class_map, class_cond, partials, send_count, recv_block):
    ngroups, ncols = lax.axis_size("rows"), lax.axis_size("cols")
    row, lanes = (CY, NZ, CX), (ROWS, NZ, LANES)
    payload = call(outgoing_kernel, (1, 0), [(ncols, SLOTS + 8, CX)])(
        send_count.reshape(ncols), partials.reshape(ncols, SLOTS, CX)
    )[0]
    incoming = lax.all_to_all(payload, "cols", split_axis=0, concat_axis=0, tiled=True)
    ids = recv_block.astype(F32).reshape(ncols * SLOTS // CX, CX)
    ids = jnp.pad(ids, ((0, 8 - ids.shape[0]), (0, 0)))
    head_t, cond_t, strip = call(fields_kernel, (1, 0, 0, 0), [row, row, (CY // 2 + 1, 8, CX)])(
        class_cond, head_start.reshape(NZ * CY, CX), class_map.reshape(NZ * CY, CX), ids
    )
    left = lax.ppermute(strip, "cols", forward(ncols))
    right = lax.ppermute(strip, "cols", backward(ncols))
    sent = (SENT, 8, CX)
    main, halo, up, down = call(recharge_kernel, (0,) * 6, [row, row, sent, sent])(
        incoming, ids, left, right, head_t, cond_t
    )
    top = lax.ppermute(down, "rows", forward(ngroups))
    bottom = lax.ppermute(up, "rows", backward(ngroups))
    place = jnp.stack([lax.axis_index("rows"), lax.axis_index("cols"), ngroups, ncols]).astype(jnp.int32)
    half = (ROWS // 2, NZ, LANES)
    head, residual = call(
        cycle_kernel, (1,) + (0,) * 8, [(NZ * CY, CX)] * 2, scratch=[lanes] * 8 + [half] * 8
    )(place, head_t, cond_t, main, halo, left, right, top, bottom)
    return head.reshape(NZ, CY, CX), residual.reshape(NZ, CY, CX)


def solution(mesh):
    placed = (
        P(None, "rows", "cols"),
        P(None, "rows", "cols"),
        P(),
        P("rows", "cols", None, None, None),
        P("rows", "cols", None),
        P("rows", "cols", None, None),
    )
    return jax.shard_map(
        body,
        mesh=mesh,
        in_specs=placed,
        out_specs=(P(None, "rows", "cols"), P(None, "rows", "cols")),
        check_vma=False,
    )
```

```python
import jax
import jax.numpy as jnp
from jax import lax
from jax.experimental import pallas as pl
from jax.experimental.pallas import tpu as pltpu
from jax.sharding import PartitionSpec as P

NZ, CY, CX, SLOTS = 8, 32, 128, 32
OMEGA = 0.8
NU1, NU2, NUC = 2, 2, 4
HY, HX = 14, 16
RY = 12
ROWS = CY + 2 * HY
LANES = 2 * CX
F32 = jnp.float32


def lane_of(shape):
    return lax.broadcasted_iota(jnp.int32, shape, len(shape) - 1)


def packed(rows, lane):
    out = None
    for q, row in enumerate(rows):
        turned = pltpu.roll(row, 32 * q + 16, 1)
        out = turned if q == 0 else jnp.where(lane // 32 == q, turned, out)
    return out


def unpacked(block, q, lane):
    turned = pltpu.roll(block, (CX - 32 * q - 16) % CX, 1)
    return jnp.where((lane < HX) | (lane >= CX - HX), turned, 0.0)


def outgoing_kernel(count_hbm, partials_hbm, out_hbm, count_ref, partials_ref, out_ref, count_sem, in_sems, out_sems):
    ncols = partials_ref.shape[0]
    part = ncols // 4
    counts = pltpu.make_async_copy(count_hbm, count_ref, count_sem)
    counts.start()
    arriving = []
    for c in range(4):
        piece = pl.ds(c * part, part)
        arriving.append(pltpu.make_async_copy(partials_hbm.at[piece], partials_ref.at[piece], in_sems.at[c]))
        arriving[c].start()
    counts.wait()
    lane = lane_of((8, CX))
    slot = lax.broadcasted_iota(jnp.int32, (8, CX), 0)
    zero = jnp.zeros((8, CX), F32)
    strips, leaving, sent = [zero], [], 0
    for d in range(ncols):
        if d % part == 0:
            arriving[d // part].wait()
        rows = []
        for q in range(SLOTS // 8):
            row = jnp.where(slot + 8 * q < count_ref[d], partials_ref[d, 8 * q : 8 * q + 8, :], 0.0)
            out_ref[d, 8 * q : 8 * q + 8, :] = row
            rows.append(row)
        strips.append(packed(rows, lane))
        if d == ncols - 1:
            strips.append(zero)
        ready = d + 1 if d == ncols - 1 else d
        for i in range(max(0, d - 1), ready):
            out_ref[i, SLOTS : SLOTS + 8, :] = jnp.where(lane % 32 < HX, strips[i], strips[i + 2])
        if d % part == part - 1:
            piece = pl.ds(sent, ready - sent)
            leaving.append(pltpu.make_async_copy(out_ref.at[piece], out_hbm.at[piece], out_sems.at[d // part]))
            leaving[-1].start()
            sent = ready
    for copy in leaving:
        copy.wait()


def fields_kernel(class_cond_ref, head_ref, class_ref, ids_ref, head_out, cond_out, strip_out):
    lane = lane_of((8, CX))
    values = [class_cond_ref[c] for c in range(8)]
    for block in range(CY // 4):
        heads, conds = [], []
        for q in range(4):
            y = 4 * block + q
            head = head_ref[pl.ds(y, NZ, stride=CY), :]
            kind = class_ref[pl.ds(y, NZ, stride=CY), :]
            cond = jnp.full((8, CX), values[0], F32)
            for c in range(1, 8):
                cond = jnp.where(kind == c, values[c], cond)
            head_out[y] = head
            cond_out[y] = cond
            heads.append(head)
            conds.append(cond)
        strip_out[block] = packed(heads, lane)
        strip_out[CY // 4 + block] = packed(conds, lane)
    strip_out[CY // 2] = ids_ref[...]


def recharge_kernel(incoming_ref, ids_ref, left_ref, right_ref, head_ref, cond_ref, main_out, halo_out, up_out, down_out):
    ncols = incoming_ref.shape[0]
    total = ncols * SLOTS
    chunk = min(256, total)
    senders = chunk // SLOTS
    lane = lane_of((8, CX))
    row = lax.broadcasted_iota(jnp.int32, (NZ * CY, chunk), 0)
    block_of = ((row % NZ) * CY + row // NZ).astype(F32)

    def onehot(ids, m):
        flat = jnp.concatenate([ids[r : r + 1, :] for r in range(m * chunk // CX, (m + 1) * chunk // CX)], axis=1)
        return jnp.where(block_of == flat, 1.0, 0.0).astype(jnp.bfloat16)

    def halves(values):
        high = values.astype(jnp.bfloat16)
        low = (values - high.astype(F32)).astype(jnp.bfloat16)
        return jnp.concatenate([high, low], axis=1)

    own, left, right = ids_ref[...], left_ref[CY // 2], right_ref[CY // 2]
    main = jnp.zeros((NZ * CY, LANES), F32)
    from_left = jnp.zeros((NZ * CY, LANES), F32)
    from_right = jnp.zeros((NZ * CY, LANES), F32)
    for m in range(total // chunk):
        values = incoming_ref[m * senders : (m + 1) * senders, 0:SLOTS, :].reshape(chunk, CX)
        main = main + jnp.dot(onehot(own, m), halves(values), preferred_element_type=F32)
        strips = []
        for s in range(m * senders, (m + 1) * senders):
            strip = incoming_ref[s, SLOTS : SLOTS + 8, :]
            strips += [pltpu.roll(strip, (CX - 32 * q - 16) % CX, 1) for q in range(4)]
        edges = halves(jnp.concatenate(strips, axis=0))
        from_left = from_left + jnp.dot(onehot(left, m), edges, preferred_element_type=F32)
        from_right = from_right + jnp.dot(onehot(right, m), edges, preferred_element_type=F32)
    main = (main[:, :CX] + main[:, CX:]).reshape(CY, NZ, CX)
    from_left = (from_left[:, :CX] + from_left[:, CX:]).reshape(CY, NZ, CX)
    from_right = (from_right[:, :CX] + from_right[:, CX:]).reshape(CY, NZ, CX)
    wide = lane_of((CY, NZ, CX))
    halo = jnp.where(wide >= CX - HX, from_left, jnp.where(wide < HX, from_right, 0.0))
    main_out[...] = main
    halo_out[...] = halo
    for out, first, strip0 in ((up_out, 0, 0), (down_out, CY - HY, CY // 4 - 4)):
        skip = first and HY - RY
        out[0:HY] = head_ref[first : first + HY]
        out[HY : 2 * HY] = cond_ref[first : first + HY]
        out[2 * HY : 2 * HY + RY] = main[first + skip : first + skip + RY]
        base = 2 * HY + RY
        for i in range(4):
            for f in range(2):
                at = f * (CY // 4) + strip0 + i
                out[base + 4 * f + i] = jnp.where(lane % 32 < HX, left_ref[at], right_ref[at])
        for i in range(RY // 4):
            y = first + skip + 4 * i
            out[base + 8 + i] = packed([halo[y + q] for q in range(4)], lane)


SENT = 2 * HY + RY + 8 + RY // 4


def span(first, last):
    return list(range(first, last + 1))


NEEDED = {
    "u0": (span(1, 58), span(14, 45)),
    "half": (span(1, 58), span(14, 45)),
    "source": (span(2, 57), span(14, 45)),
    "fx": (span(2, 57), span(14, 45)),
    "fy": (span(1, 57), span(14, 44)),
    "fz": (span(2, 57), span(14, 45)),
    "weight": (span(2, 57), span(15, 44)),
    "u1": (span(2, 57), span(15, 44)),
    "u2": (span(3, 56), span(16, 43)),
    "c_half": (span(1, 28), span(7, 22)),
    "c_fx": (span(2, 27), span(7, 22)),
    "c_fy": (span(1, 27), span(7, 21)),
    "c_fz": (span(2, 27), span(7, 22)),
    "c_weight": (span(2, 27), span(8, 21)),
    "c_source": (span(2, 27), span(9, 20)),
    "c_u0": (span(2, 27), span(9, 20)),
    "c_u1": (span(3, 26), span(10, 19)),
    "c_u2": (span(4, 25), span(11, 18)),
    "c_u3": (span(5, 24), span(12, 17)),
    "u3": (span(11, 48), span(24, 35)),
    "u4": (span(12, 47), span(25, 34)),
    "u5": (span(13, 46), span(26, 33)),
    "residual": (span(14, 45), span(27, 32)),
}
EARLY, LATE = {}, {}
for _name, (_every, _own) in NEEDED.items():
    for _r in _every:
        _into = EARLY if _r in _own else LATE
        _into[_name, _r] = len(_into)


class Cycle:
    def __init__(self, place_ref, early, late=None):
        self.early, self.late = early, late
        self.lane = lane_of((1, NZ, LANES))
        layer = lax.broadcasted_iota(jnp.int32, (1, NZ, LANES), 1)
        self.below = jnp.where(layer < NZ - 1, 1.0, 0.0)
        self.even = self.lane % 2 == 0
        g, d, ngroups, ncols = place_ref[0], place_ref[1], place_ref[2], place_ref[3]
        right = jnp.where(d < ncols - 1, CX + HX, CX)
        left = jnp.where(d > 0, LANES - HX, LANES)
        columns = jnp.where((self.lane < right) | (self.lane >= left), OMEGA, 0.0)
        above, under = jnp.where(g > 0, 1.0, 0.0), jnp.where(g < ngroups - 1, 1.0, 0.0)
        self.inside = (columns * above, columns, columns * under)

    def ranges(self, name):
        every, own = NEEDED[name]
        if self.late is None:
            return [(own[0], len(own), 1)]
        return [(every[0], own[0] - every[0], 0), (own[-1] + 1, every[-1] - own[-1], 2)]

    def get(self, name, r, n):
        parts, at = [], r
        while at < r + n:
            ref, rows = (self.early, EARLY) if (name, at) in EARLY else (self.late, LATE)
            many = 1
            while at + many < r + n and rows.get((name, at + many)) == rows[name, at] + many:
                many += 1
            parts.append(ref[pl.ds(rows[name, at], many)])
            at += many
        return parts[0] if len(parts) == 1 else jnp.concatenate(parts, axis=0)

    def put(self, name, r, n, value):
        if self.late is None:
            self.early[pl.ds(EARLY[name, r], n)] = value
        else:
            self.late[pl.ds(LATE[name, r], n)] = value

    def put_parts(self, name, r, main, halo):
        ref, at = (self.early, EARLY[name, r]) if self.late is None else (self.late, LATE[name, r])
        ref[at, :, 0:CX] = main
        ref[at, :, CX:LANES] = halo

    def turn(self, x, by):
        return pltpu.roll(x, by % LANES, 2)

    def turn_z(self, x, by):
        return pltpu.roll(x, by % NZ, 1)

    def pairs(self, x):
        two = x.reshape(x.shape[0] // 2, 2, NZ, LANES)
        two = two[:, 0] + two[:, 1]
        return two + jnp.where(self.even, self.turn(two, -1), self.turn(two, 1))

    def coefficients(self, mark, shift, zweight, own):
        for r, n, _ in self.ranges(mark + "fx"):
            k = self.get(mark + "half", r, n)
            self.put(mark + "fx", r, n, k + self.turn(k, -shift))
            self.put(mark + "fz", r, n, (k + self.turn_z(k, -1)) * (zweight * self.below))
        for r, n, _ in self.ranges(mark + "fy"):
            k = self.get(mark + "half", r, n + 1)
            self.put(mark + "fy", r, n, k[:-1] + k[1:])
        for r, n, part in self.ranges(mark + "weight"):
            pieces = [(r, n, part)]
            if part == 0:
                pieces = [(r, own[0] - r, 0), (own[0], r + n - own[0], 1)]
            elif part == 2:
                pieces = [(r, own[1] + 1 - r, 1), (own[1] + 1, r + n - own[1] - 1, 2)]
            for at, many, which in pieces:
                x, z = self.get(mark + "fx", at, many), self.get(mark + "fz", at, many)
                y = self.get(mark + "fy", at - 1, many + 1)
                total = (x + self.turn(x, shift)) + (y[1:] + y[:-1]) + (z + self.turn_z(z, 1))
                scale = self.inside[which]
                self.put(mark + "weight", at, many, scale / jnp.where(scale > 0.0, total, 1.0))

    def operator(self, u, mark, shift, r, n):
        v = self.get(u, r - 1, n + 2)
        own = v[1:-1]
        x = self.get(mark + "fx", r, n) * (own - self.turn(own, -shift))
        y = self.get(mark + "fy", r - 1, n + 1) * (v[:-1] - v[1:])
        z = self.get(mark + "fz", r, n) * (self.turn_z(own, -1) - own)
        return own, (x - self.turn(x, shift)) + (y[1:] - y[:-1]) + (z - self.turn_z(z, 1))

    def sweep(self, old, new, mark, shift):
        for r, n, _ in self.ranges(new):
            own, applied = self.operator(old, mark, shift, r, n)
            left = self.get(mark + "source", r, n) - applied
            self.put(new, r, n, own + self.get(mark + "weight", r, n) * left)

    def run(self, done):
        self.coefficients("", 1, 1.0, (HY, HY + CY - 1))
        self.sweep("u0", "u1", "", 1)
        self.sweep("u1", "u2", "", 1)
        for c, n, _ in self.ranges("c_half"):
            self.put("c_half", c, n, 0.25 * self.pairs(self.get("half", 2 * c, 2 * n)))
        self.coefficients("c_", 2, 4.0, (HY // 2, HY // 2 + CY // 2 - 1))
        for c, n, _ in self.ranges("c_source"):
            _, applied = self.operator("u2", "", 1, 2 * c, 2 * n)
            summed = self.pairs(self.get("source", 2 * c, 2 * n) - applied)
            self.put("c_source", c, n, summed)
            self.put("c_u0", c, n, self.get("c_weight", c, n) * summed)
        for i in range(1, NUC):
            self.sweep("c_u%d" % (i - 1), "c_u%d" % i, "c_", 2)
        for r, n, _ in self.ranges("u3"):
            c, many = r // 2, (r + n - 1) // 2 - r // 2 + 1
            added = self.get("c_u%d" % (NUC - 1), c, many)
            added = jnp.broadcast_to(added[:, None], (many, 2, NZ, LANES)).reshape(2 * many, NZ, LANES)
            self.put("u3", r, n, self.get("u2", r, n) + added[r % 2 : r % 2 + n])
        self.sweep("u3", "u4", "", 1)
        self.sweep("u4", "u5", "", 1)
        done()
        for r, n, _ in self.ranges("residual"):
            _, applied = self.operator("u5", "", 1, r, n)
            self.put("residual", r, n, self.get("source", r, n) - applied)


def early_kernel(place_ref, head_ref, cond_ref, main_ref, halo_ref, left_ref, right_ref, early):
    cycle = Cycle(place_ref, early)
    lane = lane_of((8, CX))
    for i in range(CY // 4):
        at = CY // 4 + i
        heads = jnp.where(lane % 32 < HX, left_ref[i], right_ref[i])
        conds = 0.5 * jnp.where(lane % 32 < HX, left_ref[at], right_ref[at])
        for q in range(4):
            y = 4 * i + q
            cycle.put_parts("u0", HY + y, head_ref[y], unpacked(heads, q, lane))
            cycle.put_parts("half", HY + y, 0.5 * cond_ref[y], unpacked(conds, q, lane))
            cycle.put_parts("source", HY + y, main_ref[y], halo_ref[y])
    cycle.run(lambda: None)


def late_kernel(place_ref, top_ref, bottom_ref, early, head_hbm, residual_hbm, late, head_ref, residual_ref, sems):
    cycle = Cycle(place_ref, early, late)
    lane = lane_of((8, CX))
    base = 2 * HY + RY
    for ref, first, shift, skip in ((top_ref, 0, 2, HY - RY), (bottom_ref, HY + CY, 0, 0)):
        for i in range(HY):
            at, q = (i + shift) // 4, (i + shift) % 4
            if first + i in NEEDED["u0"][0]:
                cycle.put_parts("u0", first + i, ref[i], unpacked(ref[base + at], q, lane))
                half = 0.5 * ref[HY + i]
                cycle.put_parts("half", first + i, half, 0.5 * unpacked(ref[base + 4 + at], q, lane))
        for i in range(RY):
            edge = unpacked(ref[base + 8 + i // 4], i % 4, lane)
            cycle.put_parts("source", first + skip + i, ref[2 * HY + i], edge)
    copies = [
        pltpu.make_async_copy(head_ref, head_hbm, sems.at[0]),
        pltpu.make_async_copy(residual_ref, residual_hbm, sems.at[1]),
    ]

    def head_done():
        for y in range(CY):
            head_ref[pl.ds(y, NZ, stride=CY), :] = cycle.get("u5", HY + y, 1)[0, :, 0:CX]
        copies[0].start()

    cycle.run(head_done)
    for y in range(CY):
        residual_ref[pl.ds(y, NZ, stride=CY), :] = cycle.get("residual", HY + y, 1)[0, :, 0:CX]
    copies[1].start()
    for copy in copies:
        copy.wait()


VMEM = pl.BlockSpec(memory_space=pltpu.VMEM)
SMEM = pl.BlockSpec(memory_space=pltpu.SMEM)
HBM = pl.BlockSpec(memory_space=pltpu.HBM)


def call(kernel, ins, outs, scratch=(), out=VMEM, limit=32 << 20, flops=1 << 20, nbytes=1 << 20):
    return pl.pallas_call(
        kernel,
        out_shape=tuple(jax.ShapeDtypeStruct(s, F32) for s in outs),
        in_specs=ins,
        out_specs=tuple(out for _ in outs),
        scratch_shapes=scratch,
        cost_estimate=pl.CostEstimate(flops=flops, bytes_accessed=nbytes, transcendentals=0),
        compiler_params=pltpu.CompilerParams(vmem_limit_bytes=limit),
    )


def forward(count):
    return [(i, i + 1) for i in range(count - 1)]


def backward(count):
    return [(i + 1, i) for i in range(count - 1)]


def early_call(place, head, cond, main, halo, left, right):
    return call(early_kernel, [SMEM] + [VMEM] * 6, [(len(EARLY), NZ, LANES)])(
        place, head, cond, main, halo, left, right
    )[0]


def late_call(place, top, bottom, early):
    flat = (NZ * CY, CX)
    scratch = [pltpu.VMEM((len(LATE), NZ, LANES), F32)] + [pltpu.VMEM(flat, F32)] * 2 + [pltpu.SemaphoreType.DMA((2,))]
    return call(late_kernel, [SMEM] + [VMEM] * 3, [flat] * 2, scratch, HBM)(place, top, bottom, early)


def body(head_start, class_map, class_cond, partials, send_count, recv_block):
    ngroups, ncols = lax.axis_size("rows"), lax.axis_size("cols")
    row, sent = (CY, NZ, CX), (SENT, 8, CX)
    scratch = [
        pltpu.SMEM((ncols,), jnp.int32),
        pltpu.VMEM((ncols, SLOTS, CX), F32),
        pltpu.VMEM((ncols, SLOTS + 8, CX), F32),
        pltpu.SemaphoreType.DMA,
        pltpu.SemaphoreType.DMA((4,)),
        pltpu.SemaphoreType.DMA((4,)),
    ]
    payload = call(outgoing_kernel, [HBM, HBM], [(ncols, SLOTS + 8, CX)], scratch, HBM, limit=64 << 20)(
        send_count.reshape(ncols), partials.reshape(ncols, SLOTS, CX)
    )[0]
    incoming = lax.all_to_all(payload, "cols", split_axis=0, concat_axis=0, tiled=True)
    ids = recv_block.astype(F32).reshape(ncols * SLOTS // CX, CX)
    ids = jnp.pad(ids, ((0, 8 - ids.shape[0]), (0, 0)))
    head, cond, strip = call(fields_kernel, [SMEM] + [VMEM] * 3, [row, row, (CY // 2 + 1, 8, CX)])(
        class_cond, head_start.reshape(NZ * CY, CX), class_map.reshape(NZ * CY, CX), ids
    )
    left = lax.ppermute(strip, "cols", forward(ncols))
    right = lax.ppermute(strip, "cols", backward(ncols))
    main, halo, up, down = call(recharge_kernel, [VMEM] * 6, [row, row, sent, sent])(
        incoming, ids, left, right, head, cond
    )
    top = lax.ppermute(down, "rows", forward(ngroups))
    bottom = lax.ppermute(up, "rows", backward(ngroups))
    place = jnp.stack([lax.axis_index("rows"), lax.axis_index("cols"), ngroups, ncols]).astype(jnp.int32)
    early = early_call(place, head, cond, main, halo, left, right)
    out = late_call(place, top, bottom, early)
    return tuple(o.reshape(NZ, CY, CX) for o in out)


def solution(mesh):
    placed = (
        P(None, "rows", "cols"),
        P(None, "rows", "cols"),
        P(),
        P("rows", "cols", None, None, None),
        P("rows", "cols", None),
        P("rows", "cols", None, None),
    )
    return jax.shard_map(
        body,
        mesh=mesh,
        in_specs=placed,
        out_specs=(P(None, "rows", "cols"), P(None, "rows", "cols")),
        check_vma=False,
    )
```

```python
import jax
import jax.numpy as jnp
from jax import lax
from jax.experimental import pallas as pl
from jax.experimental.pallas import tpu as pltpu
from jax.sharding import PartitionSpec as P

NZ, CY, CX, SLOTS, NCLASS = 8, 32, 128, 32, 8
OMEGA = 0.8
NU1, NU2, NUC = 2, 2, 4
HY, HX = 14, 16
RY = 12
ROWS = CY + 2 * HY
LANES = 2 * CX
F32 = jnp.float32


def lane_of(shape):
    return lax.broadcasted_iota(jnp.int32, shape, len(shape) - 1)


def packed(rows, lane):
    out = None
    for q, row in enumerate(rows):
        turned = pltpu.roll(row, 32 * q + 16, 1)
        out = turned if q == 0 else jnp.where(lane // 32 == q, turned, out)
    return out


def unpacked(block, q, lane):
    turned = pltpu.roll(block, (CX - 32 * q - 16) % CX, 1)
    return jnp.where((lane < HX) | (lane >= CX - HX), turned, 0.0)


def outgoing_kernel(count_hbm, partials_hbm, out_hbm, count_ref, partials_ref, out_ref, count_sem, in_sems, out_sems):
    ncols = partials_ref.shape[0]
    part = ncols // 4
    counts = pltpu.make_async_copy(count_hbm, count_ref, count_sem)
    counts.start()
    arriving = []
    for c in range(4):
        piece = pl.ds(c * part, part)
        arriving.append(pltpu.make_async_copy(partials_hbm.at[piece], partials_ref.at[piece], in_sems.at[c]))
        arriving[c].start()
    counts.wait()
    lane = lane_of((8, CX))
    slot = lax.broadcasted_iota(jnp.int32, (8, CX), 0)
    zero = jnp.zeros((8, CX), F32)
    strips, leaving, sent = [zero], [], 0
    for d in range(ncols):
        if d % part == 0:
            arriving[d // part].wait()
        rows = []
        for q in range(SLOTS // 8):
            row = jnp.where(slot + 8 * q < count_ref[d], partials_ref[d, 8 * q : 8 * q + 8, :], 0.0)
            out_ref[d, 8 * q : 8 * q + 8, :] = row
            rows.append(row)
        strips.append(packed(rows, lane))
        if d == ncols - 1:
            strips.append(zero)
        ready = d + 1 if d == ncols - 1 else d
        for i in range(max(0, d - 1), ready):
            out_ref[i, SLOTS : SLOTS + 8, :] = jnp.where(lane % 32 < HX, strips[i], strips[i + 2])
        if d % part == part - 1:
            piece = pl.ds(sent, ready - sent)
            leaving.append(pltpu.make_async_copy(out_ref.at[piece], out_hbm.at[piece], out_sems.at[d // part]))
            leaving[-1].start()
            sent = ready
    for copy in leaving:
        copy.wait()


def fields_kernel(class_cond_hbm, head_hbm, class_hbm, ids_hbm, head_out, cond_out, strip_out,
                  class_cond_ref, head_ref, class_ref, ids_ref, sems):
    pairs = (
        (head_hbm, head_ref), (class_hbm, class_ref), (class_cond_hbm, class_cond_ref), (ids_hbm, ids_ref)
    )
    copies = [pltpu.make_async_copy(a, b, sems.at[i]) for i, (a, b) in enumerate(pairs)]
    for copy in copies:
        copy.start()
    for copy in copies:
        copy.wait()
    lane = lane_of((8, CX))
    values = [class_cond_ref[c] for c in range(8)]
    for block in range(CY // 4):
        heads, conds = [], []
        for q in range(4):
            y = 4 * block + q
            head = head_ref[pl.ds(y, NZ, stride=CY), :]
            kind = class_ref[pl.ds(y, NZ, stride=CY), :]
            cond = jnp.full((8, CX), values[0], F32)
            for c in range(1, 8):
                cond = jnp.where(kind == c, values[c], cond)
            head_out[y] = head
            cond_out[y] = cond
            heads.append(head)
            conds.append(cond)
        strip_out[block] = packed(heads, lane)
        strip_out[CY // 4 + block] = packed(conds, lane)
    ids = ids_ref[...].astype(F32)
    count = ids.shape[0] // 4
    strip_out[CY // 2] = jnp.zeros((8, CX), F32)
    for r in range(count):
        strip_out[CY // 2, r : r + 1, :] = jnp.concatenate([ids[4 * r + q : 4 * r + q + 1, :] for q in range(4)], axis=1)


def rows_kernel(head_ref, cond_ref, left_ref, right_ref, up_out, down_out):
    lane = lane_of((8, CX))
    for out, first, strip0 in ((up_out, 0, 0), (down_out, CY - HY, CY // 4 - 4)):
        out[0:HY] = head_ref[first : first + HY]
        out[HY : 2 * HY] = cond_ref[first : first + HY]
        for i in range(4):
            for f in range(2):
                at = f * (CY // 4) + strip0 + i
                out[2 * HY + 4 * f + i] = jnp.where(lane % 32 < HX, left_ref[at], right_ref[at])


def recharge_kernel(incoming_ref, own_ref, left_ref, right_ref, main_out, halo_out, up_out, down_out):
    ncols = incoming_ref.shape[0]
    total = ncols * SLOTS
    chunk = min(256, total)
    senders = chunk // SLOTS
    lane = lane_of((8, CX))
    row = lax.broadcasted_iota(jnp.int32, (NZ * CY, chunk), 0)
    block_of = ((row % NZ) * CY + row // NZ).astype(F32)

    def onehot(ids, m):
        flat = jnp.concatenate([ids[r : r + 1, :] for r in range(m * chunk // CX, (m + 1) * chunk // CX)], axis=1)
        return jnp.where(block_of == flat, 1.0, 0.0).astype(jnp.bfloat16)

    def halves(values):
        high = values.astype(jnp.bfloat16)
        low = (values - high.astype(F32)).astype(jnp.bfloat16)
        return jnp.concatenate([high, low], axis=1)

    own, left, right = own_ref[CY // 2], left_ref[CY // 2], right_ref[CY // 2]
    main = jnp.zeros((NZ * CY, LANES), F32)
    from_left = jnp.zeros((NZ * CY, LANES), F32)
    from_right = jnp.zeros((NZ * CY, LANES), F32)
    for m in range(total // chunk):
        values = incoming_ref[m * senders : (m + 1) * senders, 0:SLOTS, :].reshape(chunk, CX)
        main = main + jnp.dot(onehot(own, m), halves(values), preferred_element_type=F32)
        strips = []
        for s in range(m * senders, (m + 1) * senders):
            strip = incoming_ref[s, SLOTS : SLOTS + 8, :]
            strips += [pltpu.roll(strip, (CX - 32 * q - 16) % CX, 1) for q in range(4)]
        edges = halves(jnp.concatenate(strips, axis=0))
        from_left = from_left + jnp.dot(onehot(left, m), edges, preferred_element_type=F32)
        from_right = from_right + jnp.dot(onehot(right, m), edges, preferred_element_type=F32)
    main = (main[:, :CX] + main[:, CX:]).reshape(CY, NZ, CX)
    from_left = (from_left[:, :CX] + from_left[:, CX:]).reshape(CY, NZ, CX)
    from_right = (from_right[:, :CX] + from_right[:, CX:]).reshape(CY, NZ, CX)
    wide = lane_of((CY, NZ, CX))
    halo = jnp.where(wide >= CX - HX, from_left, jnp.where(wide < HX, from_right, 0.0))
    main_out[...] = main
    halo_out[...] = halo
    for out, first in ((up_out, 0), (down_out, CY - RY)):
        out[0:RY] = main[first : first + RY]
        for i in range(RY // 4):
            y = first + 4 * i
            out[RY + i] = packed([halo[y + q] for q in range(4)], lane)


FIELD_ROWS, RECHARGE_ROWS = 2 * HY + 8, RY + RY // 4


def span(first, last):
    return list(range(first, last + 1))


NEEDED = {
    "u0": (span(1, 58), span(1, 58)),
    "half": (span(1, 58), span(1, 58)),
    "source": (span(2, 57), span(14, 45)),
    "fx": (span(2, 57), span(2, 57)),
    "fy": (span(1, 57), span(1, 57)),
    "fz": (span(2, 57), span(2, 57)),
    "weight": (span(2, 57), span(2, 57)),
    "above": (span(2, 14), span(2, 14)),
    "below": (span(45, 57), span(45, 57)),
    "u1": (span(2, 57), span(15, 44)),
    "u2": (span(3, 56), span(16, 43)),
    "c_half": (span(1, 28), span(1, 28)),
    "c_fx": (span(2, 27), span(2, 27)),
    "c_fy": (span(1, 27), span(1, 27)),
    "c_fz": (span(2, 27), span(2, 27)),
    "c_weight": (span(2, 27), span(2, 27)),
    "c_source": (span(2, 27), span(9, 20)),
    "c_u0": (span(2, 27), span(9, 20)),
    "c_u1": (span(3, 26), span(10, 19)),
    "c_u2": (span(4, 25), span(11, 18)),
    "c_u3": (span(5, 24), span(12, 17)),
    "u3": (span(11, 48), span(24, 35)),
    "u4": (span(12, 47), span(25, 34)),
    "u5": (span(13, 46), span(26, 33)),
    "residual": (span(14, 45), span(27, 32)),
}
EARLY, LATE = {}, {}
for _name, (_every, _own) in NEEDED.items():
    for _r in _every:
        _into = EARLY if _r in _own else LATE
        _into[_name, _r] = len(_into)


class Cycle:
    def __init__(self, place_ref, early, late=None):
        self.early, self.late = early, late
        self.lane = lane_of((1, NZ, LANES))
        layer = lax.broadcasted_iota(jnp.int32, (1, NZ, LANES), 1)
        self.below = jnp.where(layer < NZ - 1, 1.0, 0.0)
        self.even = self.lane % 2 == 0
        g, d, ngroups, ncols = place_ref[0], place_ref[1], place_ref[2], place_ref[3]
        right = jnp.where(d < ncols - 1, CX + HX, CX)
        left = jnp.where(d > 0, LANES - HX, LANES)
        columns = jnp.where((self.lane < right) | (self.lane >= left), OMEGA, 0.0)
        above, under = jnp.where(g > 0, 1.0, 0.0), jnp.where(g < ngroups - 1, 1.0, 0.0)
        self.inside = (columns * above, columns, columns * under)

    def ranges(self, name):
        every, own = NEEDED[name]
        if self.late is None:
            return [(own[0], len(own))]
        return [(every[0], own[0] - every[0]), (own[-1] + 1, every[-1] - own[-1])]

    def get(self, name, r, n):
        parts, at = [], r
        while at < r + n:
            ref, rows = (self.early, EARLY) if (name, at) in EARLY else (self.late, LATE)
            many = 1
            while at + many < r + n and rows.get((name, at + many)) == rows[name, at] + many:
                many += 1
            parts.append(ref[pl.ds(rows[name, at], many)])
            at += many
        return parts[0] if len(parts) == 1 else jnp.concatenate(parts, axis=0)

    def put(self, name, r, n, value):
        if self.late is None:
            self.early[pl.ds(EARLY[name, r], n)] = value
        else:
            self.late[pl.ds(LATE[name, r], n)] = value

    def put_parts(self, name, r, main, halo):
        ref, at = (self.early, EARLY[name, r]) if self.late is None else (self.late, LATE[name, r])
        ref[at, :, 0:CX] = main
        ref[at, :, CX:LANES] = halo

    def turn(self, x, by):
        return pltpu.roll(x, by % LANES, 2)

    def turn_z(self, x, by):
        return pltpu.roll(x, by % NZ, 1)

    def pairs(self, x):
        two = x.reshape(x.shape[0] // 2, 2, NZ, LANES)
        two = two[:, 0] + two[:, 1]
        return two + jnp.where(self.even, self.turn(two, -1), self.turn(two, 1))

    def coefficients(self, mark, shift, zweight, own):
        r, n = self.ranges(mark + "fx")[0]
        k = self.get(mark + "half", r, n)
        self.put(mark + "fx", r, n, k + self.turn(k, -shift))
        self.put(mark + "fz", r, n, (k + self.turn_z(k, -1)) * (zweight * self.below))
        r, n = self.ranges(mark + "fy")[0]
        k = self.get(mark + "half", r, n + 1)
        self.put(mark + "fy", r, n, k[:-1] + k[1:])
        r, n = self.ranges(mark + "weight")[0]
        for at, end, scale in zip((r,) + own, own + (r + n,), self.inside):
            many = end - at
            x, z = self.get(mark + "fx", at, many), self.get(mark + "fz", at, many)
            y = self.get(mark + "fy", at - 1, many + 1)
            total = (x + self.turn(x, shift)) + (y[1:] + y[:-1]) + (z + self.turn_z(z, 1))
            self.put(mark + "weight", at, many, scale / jnp.where(scale > 0.0, total, 1.0))

    def operator(self, u, mark, shift, r, n):
        v = self.get(u, r - 1, n + 2)
        own = v[1:-1]
        x = self.get(mark + "fx", r, n) * (own - self.turn(own, -shift))
        y = self.get(mark + "fy", r - 1, n + 1) * (v[:-1] - v[1:])
        z = self.get(mark + "fz", r, n) * (self.turn_z(own, -1) - own)
        return own, (x - self.turn(x, shift)) + (y[1:] - y[:-1]) + (z - self.turn_z(z, 1))

    def sweep(self, old, new, mark, shift):
        for r, n in self.ranges(new):
            own, applied = self.operator(old, mark, shift, r, n)
            left = self.get(mark + "source", r, n) - applied
            self.put(new, r, n, own + self.get(mark + "weight", r, n) * left)

    def run(self, done):
        if self.late is None:
            self.coefficients("", 1, 1.0, (HY, HY + CY))
            self.sweep("u0", "u1", "", 1)
            c, n = self.ranges("c_half")[0]
            self.put("c_half", c, n, 0.25 * self.pairs(self.get("half", 2 * c, 2 * n)))
            self.coefficients("c_", 2, 4.0, (HY // 2, HY // 2 + CY // 2))
            for name in ("above", "below"):
                r, n = self.ranges(name)[0]
                own, applied = self.operator("u0", "", 1, r, n)
                self.put(name, r, n, own - self.get("weight", r, n) * applied)
        else:
            for name, (r, n) in zip(("above", "below"), self.ranges("u1")):
                added = self.get("weight", r, n) * self.get("source", r, n)
                self.put("u1", r, n, self.get(name, r, n) + added)
        self.sweep("u1", "u2", "", 1)
        for c, n in self.ranges("c_source"):
            _, applied = self.operator("u2", "", 1, 2 * c, 2 * n)
            summed = self.pairs(self.get("source", 2 * c, 2 * n) - applied)
            self.put("c_source", c, n, summed)
            self.put("c_u0", c, n, self.get("c_weight", c, n) * summed)
        for i in range(1, NUC):
            self.sweep("c_u%d" % (i - 1), "c_u%d" % i, "c_", 2)
        for r, n in self.ranges("u3"):
            c, many = r // 2, (r + n - 1) // 2 - r // 2 + 1
            added = self.get("c_u%d" % (NUC - 1), c, many)
            added = jnp.broadcast_to(added[:, None], (many, 2, NZ, LANES)).reshape(2 * many, NZ, LANES)
            self.put("u3", r, n, self.get("u2", r, n) + added[r % 2 : r % 2 + n])
        self.sweep("u3", "u4", "", 1)
        self.sweep("u4", "u5", "", 1)
        done()
        for r, n in self.ranges("residual"):
            _, applied = self.operator("u5", "", 1, r, n)
            self.put("residual", r, n, self.get("source", r, n) - applied)


def early_kernel(place_ref, head_ref, cond_ref, main_ref, halo_ref, left_ref, right_ref, top_ref, bottom_ref, early):
    cycle = Cycle(place_ref, early)
    lane = lane_of((8, CX))
    for i in range(CY // 4):
        at = CY // 4 + i
        heads = jnp.where(lane % 32 < HX, left_ref[i], right_ref[i])
        conds = 0.5 * jnp.where(lane % 32 < HX, left_ref[at], right_ref[at])
        for q in range(4):
            y = 4 * i + q
            cycle.put_parts("u0", HY + y, head_ref[y], unpacked(heads, q, lane))
            cycle.put_parts("half", HY + y, 0.5 * cond_ref[y], unpacked(conds, q, lane))
            cycle.put_parts("source", HY + y, main_ref[y], halo_ref[y])
    for ref, first, shift in ((top_ref, 0, 2), (bottom_ref, HY + CY, 0)):
        for i in range(HY):
            at, q = (i + shift) // 4, (i + shift) % 4
            if first + i in NEEDED["u0"][0]:
                cycle.put_parts("u0", first + i, ref[i], unpacked(ref[2 * HY + at], q, lane))
                half = 0.5 * ref[HY + i]
                cycle.put_parts("half", first + i, half, 0.5 * unpacked(ref[2 * HY + 4 + at], q, lane))
    cycle.run(lambda: None)


def late_kernel(place_ref, top_ref, bottom_ref, early, head_hbm, residual_hbm, late, head_ref, residual_ref, sems):
    cycle = Cycle(place_ref, early, late)
    lane = lane_of((8, CX))
    for ref, first in ((top_ref, HY - RY), (bottom_ref, HY + CY)):
        for i in range(RY):
            cycle.put_parts("source", first + i, ref[i], unpacked(ref[RY + i // 4], i % 4, lane))
    copies = [
        pltpu.make_async_copy(head_ref, head_hbm, sems.at[0]),
        pltpu.make_async_copy(residual_ref, residual_hbm, sems.at[1]),
    ]

    def head_done():
        for y in range(CY):
            head_ref[pl.ds(y, NZ, stride=CY), :] = cycle.get("u5", HY + y, 1)[0, :, 0:CX]
        copies[0].start()

    cycle.run(head_done)
    for y in range(CY):
        residual_ref[pl.ds(y, NZ, stride=CY), :] = cycle.get("residual", HY + y, 1)[0, :, 0:CX]
    copies[1].start()
    for copy in copies:
        copy.wait()


VMEM = pl.BlockSpec(memory_space=pltpu.VMEM)
SMEM = pl.BlockSpec(memory_space=pltpu.SMEM)
HBM = pl.BlockSpec(memory_space=pltpu.HBM)


def in_hbm(x):
    return pltpu.with_memory_space_constraint(x, pltpu.HBM)


def call(kernel, ins, outs, scratch=(), out=VMEM, flops=1 << 20, nbytes=1 << 20):
    return pl.pallas_call(
        kernel,
        out_shape=tuple(jax.ShapeDtypeStruct(s, F32) for s in outs),
        in_specs=ins,
        out_specs=tuple(out for _ in outs),
        scratch_shapes=scratch,
        cost_estimate=pl.CostEstimate(flops=flops, bytes_accessed=nbytes, transcendentals=0),
        compiler_params=pltpu.CompilerParams(vmem_limit_bytes=32 << 20),
    )


def forward(count):
    return [(i, i + 1) for i in range(count - 1)]


def backward(count):
    return [(i + 1, i) for i in range(count - 1)]


def early_call(place, head, cond, main, halo, left, right, top, bottom):
    return call(early_kernel, [SMEM] + [VMEM] * 8, [(len(EARLY), NZ, LANES)])(
        place, head, cond, main, halo, left, right, top, bottom
    )[0]


def late_call(place, top, bottom, early):
    flat = (NZ * CY, CX)
    scratch = [pltpu.VMEM((len(LATE), NZ, LANES), F32)] + [pltpu.VMEM(flat, F32)] * 2 + [pltpu.SemaphoreType.DMA((2,))]
    return call(late_kernel, [SMEM] + [VMEM] * 3, [flat] * 2, scratch, HBM)(place, top, bottom, early)


def body(head_start, class_map, class_cond, partials, send_count, recv_block):
    ngroups, ncols = lax.axis_size("rows"), lax.axis_size("cols")
    row = (CY, NZ, CX)
    scratch = [
        pltpu.SMEM((ncols,), jnp.int32),
        pltpu.VMEM((ncols, SLOTS, CX), F32),
        pltpu.VMEM((ncols, SLOTS + 8, CX), F32),
        pltpu.SemaphoreType.DMA,
        pltpu.SemaphoreType.DMA((4,)),
        pltpu.SemaphoreType.DMA((4,)),
    ]
    payload = call(outgoing_kernel, [HBM, HBM], [(ncols, SLOTS + 8, CX)], scratch, HBM)(
        in_hbm(send_count.reshape(ncols)), in_hbm(partials.reshape(ncols, SLOTS, CX))
    )[0]
    incoming = lax.all_to_all(payload, "cols", split_axis=0, concat_axis=0, tiled=True)
    flat = (NZ * CY, CX)
    scratch = [
        pltpu.SMEM((NCLASS,), F32),
        pltpu.VMEM(flat, F32),
        pltpu.VMEM(flat, jnp.int32),
        pltpu.VMEM((ncols, SLOTS), jnp.int32),
        pltpu.SemaphoreType.DMA((4,)),
    ]
    head, cond, strip = call(fields_kernel, [HBM] * 4, [row, row, (CY // 2 + 1, 8, CX)], scratch)(
        *(in_hbm(x) for x in (class_cond, head_start.reshape(flat), class_map.reshape(flat), recv_block.reshape(ncols, SLOTS)))
    )
    left = lax.ppermute(strip, "cols", forward(ncols))
    right = lax.ppermute(strip, "cols", backward(ncols))
    up, down = call(rows_kernel, [VMEM] * 4, [(FIELD_ROWS, 8, CX)] * 2)(head, cond, left, right)
    top = lax.ppermute(down, "rows", forward(ngroups))
    bottom = lax.ppermute(up, "rows", backward(ngroups))
    main, halo, up, down = call(recharge_kernel, [VMEM] * 4, [row, row] + [(RECHARGE_ROWS, 8, CX)] * 2)(
        incoming, strip, left, right
    )
    top_source = lax.ppermute(down, "rows", forward(ngroups))
    bottom_source = lax.ppermute(up, "rows", backward(ngroups))
    place = jnp.stack([lax.axis_index("rows"), lax.axis_index("cols"), ngroups, ncols]).astype(jnp.int32)
    early = early_call(place, head, cond, main, halo, left, right, top, bottom)
    out = late_call(place, top_source, bottom_source, early)
    return tuple(o.reshape(NZ, CY, CX) for o in out)


def solution(mesh):
    placed = (
        P(None, "rows", "cols"),
        P(None, "rows", "cols"),
        P(),
        P("rows", "cols", None, None, None),
        P("rows", "cols", None),
        P("rows", "cols", None, None),
    )
    return jax.shard_map(
        body,
        mesh=mesh,
        in_specs=placed,
        out_specs=(P(None, "rows", "cols"), P(None, "rows", "cols")),
        check_vma=False,
    )
```

```python
import functools

import jax
import jax.numpy as jnp
from jax import lax
from jax.experimental import pallas as pl
from jax.experimental.pallas import tpu as pltpu
from jax.sharding import PartitionSpec as P

NZ, CY, CX, SLOTS, NCLASS = 8, 32, 128, 32, 8
OMEGA = 0.8
NU1, NU2, NUC = 2, 2, 4
HY, HX = 14, 16
RY = 12
ROWS = CY + 2 * HY
LANES = 2 * CX
F32 = jnp.float32


def lane_of(shape):
    return lax.broadcasted_iota(jnp.int32, shape, len(shape) - 1)


def packed(rows, lane):
    out = None
    for q, row in enumerate(rows):
        turned = pltpu.roll(row, 32 * q + 16, 1)
        out = turned if q == 0 else jnp.where(lane // 32 == q, turned, out)
    return out


def unpacked(block, q, lane):
    turned = pltpu.roll(block, (CX - 32 * q - 16) % CX, 1)
    return jnp.where((lane < HX) | (lane >= CX - HX), turned, 0.0)


def outgoing_kernel(count_hbm, partials_hbm, out_hbm, count_ref, partials_ref, out_ref, count_sem, in_sems, out_sems):
    ncols = partials_ref.shape[0]
    part = ncols // 4
    counts = pltpu.make_async_copy(count_hbm, count_ref, count_sem)
    counts.start()
    arriving = []
    for c in range(4):
        piece = pl.ds(c * part, part)
        arriving.append(pltpu.make_async_copy(partials_hbm.at[piece], partials_ref.at[piece], in_sems.at[c]))
        arriving[c].start()
    counts.wait()
    lane = lane_of((8, CX))
    slot = lax.broadcasted_iota(jnp.int32, (8, CX), 0)
    zero = jnp.zeros((8, CX), F32)
    strips, leaving, sent = [zero], [], 0
    for d in range(ncols):
        if d % part == 0:
            arriving[d // part].wait()
        rows = []
        for q in range(SLOTS // 8):
            row = jnp.where(slot + 8 * q < count_ref[d], partials_ref[d, 8 * q : 8 * q + 8, :], 0.0)
            out_ref[d, 8 * q : 8 * q + 8, :] = row
            rows.append(row)
        strips.append(packed(rows, lane))
        if d == ncols - 1:
            strips.append(zero)
        ready = d + 1 if d == ncols - 1 else d
        for i in range(max(0, d - 1), ready):
            out_ref[i, SLOTS : SLOTS + 8, :] = jnp.where(lane % 32 < HX, strips[i], strips[i + 2])
        if d % part == part - 1:
            piece = pl.ds(sent, ready - sent)
            leaving.append(pltpu.make_async_copy(out_ref.at[piece], out_hbm.at[piece], out_sems.at[d // part]))
            leaving[-1].start()
            sent = ready
    for copy in leaving:
        copy.wait()


def fields_kernel(class_cond_hbm, head_hbm, class_hbm, ids_hbm, head_out, cond_out, strip_out,
                  class_cond_ref, head_ref, class_ref, ids_ref, sems):
    pairs = (
        (head_hbm, head_ref), (class_hbm, class_ref), (class_cond_hbm, class_cond_ref), (ids_hbm, ids_ref)
    )
    copies = [pltpu.make_async_copy(a, b, sems.at[i]) for i, (a, b) in enumerate(pairs)]
    for copy in copies:
        copy.start()
    for copy in copies:
        copy.wait()
    lane = lane_of((8, CX))
    values = [class_cond_ref[c] for c in range(8)]
    for block in range(CY // 4):
        heads, conds = [], []
        for q in range(4):
            y = 4 * block + q
            head = head_ref[pl.ds(y, NZ, stride=CY), :]
            kind = class_ref[pl.ds(y, NZ, stride=CY), :]
            cond = jnp.full((8, CX), values[0], F32)
            for c in range(1, 8):
                cond = jnp.where(kind == c, values[c], cond)
            head_out[y] = head
            cond_out[y] = cond
            heads.append(head)
            conds.append(cond)
        strip_out[block] = packed(heads, lane)
        strip_out[CY // 4 + block] = packed(conds, lane)
    ids = ids_ref[...].astype(F32)
    count = ids.shape[0] // 4
    strip_out[CY // 2] = jnp.zeros((8, CX), F32)
    for r in range(count):
        strip_out[CY // 2, r : r + 1, :] = jnp.concatenate([ids[4 * r + q : 4 * r + q + 1, :] for q in range(4)], axis=1)


def recharge_kernel(incoming_ref, own_ref, left_ref, right_ref, head_ref, cond_ref, main_out, halo_out, up_out, down_out):
    ncols = incoming_ref.shape[0]
    total = ncols * SLOTS
    chunk = min(256, total)
    senders = chunk // SLOTS
    lane = lane_of((8, CX))
    row = lax.broadcasted_iota(jnp.int32, (NZ * CY, chunk), 0)
    block_of = ((row % NZ) * CY + row // NZ).astype(F32)

    def onehot(ids, m):
        flat = jnp.concatenate([ids[r : r + 1, :] for r in range(m * chunk // CX, (m + 1) * chunk // CX)], axis=1)
        return jnp.where(block_of == flat, 1.0, 0.0).astype(jnp.bfloat16)

    def halves(values):
        high = values.astype(jnp.bfloat16)
        low = (values - high.astype(F32)).astype(jnp.bfloat16)
        return jnp.concatenate([high, low], axis=1)

    own, left, right = own_ref[CY // 2], left_ref[CY // 2], right_ref[CY // 2]
    main = jnp.zeros((NZ * CY, LANES), F32)
    from_left = jnp.zeros((NZ * CY, LANES), F32)
    from_right = jnp.zeros((NZ * CY, LANES), F32)
    for m in range(total // chunk):
        values = incoming_ref[m * senders : (m + 1) * senders, 0:SLOTS, :].reshape(chunk, CX)
        main = main + jnp.dot(onehot(own, m), halves(values), preferred_element_type=F32)
        strips = []
        for s in range(m * senders, (m + 1) * senders):
            strip = incoming_ref[s, SLOTS : SLOTS + 8, :]
            strips += [pltpu.roll(strip, (CX - 32 * q - 16) % CX, 1) for q in range(4)]
        edges = halves(jnp.concatenate(strips, axis=0))
        from_left = from_left + jnp.dot(onehot(left, m), edges, preferred_element_type=F32)
        from_right = from_right + jnp.dot(onehot(right, m), edges, preferred_element_type=F32)
    main = (main[:, :CX] + main[:, CX:]).reshape(CY, NZ, CX)
    from_left = (from_left[:, :CX] + from_left[:, CX:]).reshape(CY, NZ, CX)
    from_right = (from_right[:, :CX] + from_right[:, CX:]).reshape(CY, NZ, CX)
    wide = lane_of((CY, NZ, CX))
    halo = jnp.where(wide >= CX - HX, from_left, jnp.where(wide < HX, from_right, 0.0))
    main_out[...] = main
    halo_out[...] = halo
    for out, first, strip0 in ((up_out, 0, 0), (down_out, CY - HY, CY // 4 - 4)):
        skip = first and HY - RY
        out[0:HY] = head_ref[first : first + HY]
        out[HY : 2 * HY] = cond_ref[first : first + HY]
        out[2 * HY : 2 * HY + RY] = main[first + skip : first + skip + RY]
        base = 2 * HY + RY
        for i in range(4):
            for f in range(2):
                at = f * (CY // 4) + strip0 + i
                out[base + 4 * f + i] = jnp.where(lane % 32 < HX, left_ref[at], right_ref[at])
        for i in range(RY // 4):
            y = first + skip + 4 * i
            out[base + 8 + i] = packed([halo[y + q] for q in range(4)], lane)


SENT = 2 * HY + RY + 8 + RY // 4


def span(first, last):
    return list(range(first, last + 1))


NEEDED = {
    "u0": (span(1, 58), span(14, 45)),
    "half": (span(1, 58), span(14, 45)),
    "source": (span(2, 57), span(14, 45)),
    "fx": (span(2, 57), span(14, 45)),
    "fy": (span(1, 57), span(14, 44)),
    "fz": (span(2, 57), span(14, 45)),
    "weight": (span(2, 57), span(15, 44)),
    "u1": (span(2, 57), span(15, 44)),
    "u2": (span(3, 56), span(16, 43)),
    "c_half": (span(1, 28), span(7, 22)),
    "c_fx": (span(2, 27), span(7, 22)),
    "c_fy": (span(1, 27), span(7, 21)),
    "c_fz": (span(2, 27), span(7, 22)),
    "c_weight": (span(2, 27), span(8, 21)),
    "c_source": (span(2, 27), span(9, 20)),
    "c_u0": (span(2, 27), span(9, 20)),
    "c_u1": (span(3, 26), span(10, 19)),
    "c_u2": (span(4, 25), span(11, 18)),
    "c_u3": (span(5, 24), span(12, 17)),
    "u3": (span(11, 48), span(24, 35)),
    "u4": (span(12, 47), span(25, 34)),
    "u5": (span(13, 46), span(26, 33)),
    "residual": (span(14, 45), span(27, 32)),
}
EARLY, LATE = {}, ({}, {})
for _name, (_every, _own) in NEEDED.items():
    for _r in _every:
        _into = EARLY if _r in _own else LATE[0 if _r < _own[0] else 1]
        _into[_name, _r] = len(_into)


class Cycle:
    def __init__(self, place_ref, early, late=None, side=None):
        self.early, self.late, self.side = early, late, side
        self.lane = lane_of((1, NZ, LANES))
        layer = lax.broadcasted_iota(jnp.int32, (1, NZ, LANES), 1)
        self.below = jnp.where(layer < NZ - 1, 1.0, 0.0)
        self.even = self.lane % 2 == 0
        g, d, ngroups, ncols = place_ref[0], place_ref[1], place_ref[2], place_ref[3]
        right = jnp.where(d < ncols - 1, CX + HX, CX)
        left = jnp.where(d > 0, LANES - HX, LANES)
        columns = jnp.where((self.lane < right) | (self.lane >= left), OMEGA, 0.0)
        above, under = jnp.where(g > 0, 1.0, 0.0), jnp.where(g < ngroups - 1, 1.0, 0.0)
        self.inside = (columns * above, columns, columns * under)

    def ranges(self, name):
        every, own = NEEDED[name]
        if self.late is None:
            return [(own[0], len(own), 1)]
        if self.side == 0:
            return [(every[0], own[0] - every[0], 0)]
        return [(own[-1] + 1, every[-1] - own[-1], 2)]

    def get(self, name, r, n):
        parts, at = [], r
        while at < r + n:
            ref, rows = (self.early, EARLY) if (name, at) in EARLY else (self.late, LATE[self.side])
            many = 1
            while at + many < r + n and rows.get((name, at + many)) == rows[name, at] + many:
                many += 1
            parts.append(ref[pl.ds(rows[name, at], many)])
            at += many
        return parts[0] if len(parts) == 1 else jnp.concatenate(parts, axis=0)

    def put(self, name, r, n, value):
        if self.late is None:
            self.early[pl.ds(EARLY[name, r], n)] = value
        else:
            self.late[pl.ds(LATE[self.side][name, r], n)] = value

    def put_parts(self, name, r, main, halo):
        ref, at = (self.early, EARLY[name, r]) if self.late is None else (self.late, LATE[self.side][name, r])
        ref[at, :, 0:CX] = main
        ref[at, :, CX:LANES] = halo

    def turn(self, x, by):
        return pltpu.roll(x, by % LANES, 2)

    def turn_z(self, x, by):
        return pltpu.roll(x, by % NZ, 1)

    def pairs(self, x):
        two = x.reshape(x.shape[0] // 2, 2, NZ, LANES)
        two = two[:, 0] + two[:, 1]
        return two + jnp.where(self.even, self.turn(two, -1), self.turn(two, 1))

    def coefficients(self, mark, shift, zweight, own):
        for r, n, _ in self.ranges(mark + "fx"):
            k = self.get(mark + "half", r, n)
            self.put(mark + "fx", r, n, k + self.turn(k, -shift))
            self.put(mark + "fz", r, n, (k + self.turn_z(k, -1)) * (zweight * self.below))
        for r, n, _ in self.ranges(mark + "fy"):
            k = self.get(mark + "half", r, n + 1)
            self.put(mark + "fy", r, n, k[:-1] + k[1:])
        for r, n, part in self.ranges(mark + "weight"):
            pieces = [(r, n, part)]
            if part == 0:
                pieces = [(r, own[0] - r, 0), (own[0], r + n - own[0], 1)]
            elif part == 2:
                pieces = [(r, own[1] + 1 - r, 1), (own[1] + 1, r + n - own[1] - 1, 2)]
            for at, many, which in pieces:
                x, z = self.get(mark + "fx", at, many), self.get(mark + "fz", at, many)
                y = self.get(mark + "fy", at - 1, many + 1)
                total = (x + self.turn(x, shift)) + (y[1:] + y[:-1]) + (z + self.turn_z(z, 1))
                scale = self.inside[which]
                self.put(mark + "weight", at, many, scale / jnp.where(scale > 0.0, total, 1.0))

    def operator(self, u, mark, shift, r, n):
        v = self.get(u, r - 1, n + 2)
        own = v[1:-1]
        x = self.get(mark + "fx", r, n) * (own - self.turn(own, -shift))
        y = self.get(mark + "fy", r - 1, n + 1) * (v[:-1] - v[1:])
        z = self.get(mark + "fz", r, n) * (self.turn_z(own, -1) - own)
        return own, (x - self.turn(x, shift)) + (y[1:] - y[:-1]) + (z - self.turn_z(z, 1))

    def sweep(self, old, new, mark, shift):
        for r, n, _ in self.ranges(new):
            own, applied = self.operator(old, mark, shift, r, n)
            left = self.get(mark + "source", r, n) - applied
            self.put(new, r, n, own + self.get(mark + "weight", r, n) * left)

    def run(self, done):
        self.coefficients("", 1, 1.0, (HY, HY + CY - 1))
        self.sweep("u0", "u1", "", 1)
        self.sweep("u1", "u2", "", 1)
        for c, n, _ in self.ranges("c_half"):
            self.put("c_half", c, n, 0.25 * self.pairs(self.get("half", 2 * c, 2 * n)))
        self.coefficients("c_", 2, 4.0, (HY // 2, HY // 2 + CY // 2 - 1))
        for c, n, _ in self.ranges("c_source"):
            _, applied = self.operator("u2", "", 1, 2 * c, 2 * n)
            summed = self.pairs(self.get("source", 2 * c, 2 * n) - applied)
            self.put("c_source", c, n, summed)
            self.put("c_u0", c, n, self.get("c_weight", c, n) * summed)
        for i in range(1, NUC):
            self.sweep("c_u%d" % (i - 1), "c_u%d" % i, "c_", 2)
        for r, n, _ in self.ranges("u3"):
            c, many = r // 2, (r + n - 1) // 2 - r // 2 + 1
            added = self.get("c_u%d" % (NUC - 1), c, many)
            added = jnp.broadcast_to(added[:, None], (many, 2, NZ, LANES)).reshape(2 * many, NZ, LANES)
            self.put("u3", r, n, self.get("u2", r, n) + added[r % 2 : r % 2 + n])
        self.sweep("u3", "u4", "", 1)
        self.sweep("u4", "u5", "", 1)
        done()
        for r, n, _ in self.ranges("residual"):
            _, applied = self.operator("u5", "", 1, r, n)
            self.put("residual", r, n, self.get("source", r, n) - applied)


def early_kernel(place_ref, head_ref, cond_ref, main_ref, halo_ref, left_ref, right_ref, early):
    cycle = Cycle(place_ref, early)
    lane = lane_of((8, CX))
    for i in range(CY // 4):
        at = CY // 4 + i
        heads = jnp.where(lane % 32 < HX, left_ref[i], right_ref[i])
        conds = 0.5 * jnp.where(lane % 32 < HX, left_ref[at], right_ref[at])
        for q in range(4):
            y = 4 * i + q
            cycle.put_parts("u0", HY + y, head_ref[y], unpacked(heads, q, lane))
            cycle.put_parts("half", HY + y, 0.5 * cond_ref[y], unpacked(conds, q, lane))
            cycle.put_parts("source", HY + y, main_ref[y], halo_ref[y])
    cycle.run(lambda: None)


def late_kernel(side, place_ref, sent_ref, early, *refs):
    head_hbm, residual_hbm, late, head_ref, residual_ref, sems = refs[-6:]
    cycle = Cycle(place_ref, early, late, side)
    lane = lane_of((8, CX))
    base = 2 * HY + RY
    first, shift, skip = ((0, 2, HY - RY), (HY + CY, 0, 0))[side]
    for i in range(HY):
        at, q = (i + shift) // 4, (i + shift) % 4
        if first + i in NEEDED["u0"][0]:
            cycle.put_parts("u0", first + i, sent_ref[i], unpacked(sent_ref[base + at], q, lane))
            half = 0.5 * sent_ref[HY + i]
            cycle.put_parts("half", first + i, half, 0.5 * unpacked(sent_ref[base + 4 + at], q, lane))
    for i in range(RY):
        edge = unpacked(sent_ref[base + 8 + i // 4], i % 4, lane)
        cycle.put_parts("source", first + skip + i, sent_ref[2 * HY + i], edge)
    own = pl.ds(side * (CY // 2), CY // 2)
    copies = [
        pltpu.make_async_copy(head_ref, head_hbm.at[:, own, :], sems.at[0]),
        pltpu.make_async_copy(residual_ref, residual_hbm.at[:, own, :], sems.at[1]),
    ]

    def leave(name, ref):
        for y in range(CY // 2):
            ref[:, y, :] = cycle.get(name, HY + side * (CY // 2) + y, 1)[0, :, 0:CX]

    def head_done():
        leave("u5", head_ref)
        copies[0].start()

    cycle.run(head_done)
    leave("residual", residual_ref)
    copies[1].start()
    for copy in copies:
        copy.wait()


VMEM = pl.BlockSpec(memory_space=pltpu.VMEM)
SMEM = pl.BlockSpec(memory_space=pltpu.SMEM)
HBM = pl.BlockSpec(memory_space=pltpu.HBM)


def in_hbm(x):
    return pltpu.with_memory_space_constraint(x, pltpu.HBM)


def call(kernel, ins, outs, scratch=(), out=VMEM, aliases={}, flops=1 << 20, nbytes=1 << 20):
    return pl.pallas_call(
        kernel,
        out_shape=tuple(jax.ShapeDtypeStruct(s, F32) for s in outs),
        in_specs=ins,
        out_specs=tuple(out for _ in outs),
        scratch_shapes=scratch,
        input_output_aliases=aliases,
        cost_estimate=pl.CostEstimate(flops=flops, bytes_accessed=nbytes, transcendentals=0),
        compiler_params=pltpu.CompilerParams(vmem_limit_bytes=32 << 20),
    )


def forward(count):
    return [(i, i + 1) for i in range(count - 1)]


def backward(count):
    return [(i + 1, i) for i in range(count - 1)]


def early_call(place, head, cond, main, halo, left, right):
    return call(early_kernel, [SMEM] + [VMEM] * 6, [(len(EARLY), NZ, LANES)])(
        place, head, cond, main, halo, left, right
    )[0]


def late_call(side, place, sent, early, outs=()):
    half = pltpu.VMEM((NZ, CY // 2, CX), F32)
    return call(
        functools.partial(late_kernel, side),
        [SMEM] + [VMEM] * 2 + [HBM] * len(outs),
        [(NZ, CY, CX)] * 2,
        [pltpu.VMEM((len(LATE[side]), NZ, LANES), F32), half, half, pltpu.SemaphoreType.DMA((2,))],
        HBM,
        {3: 0, 4: 1} if outs else {},
    )(place, sent, early, *outs)


def body(head_start, class_map, class_cond, partials, send_count, recv_block):
    ngroups, ncols = lax.axis_size("rows"), lax.axis_size("cols")
    row, sent = (CY, NZ, CX), (SENT, 8, CX)
    scratch = [
        pltpu.SMEM((ncols,), jnp.int32),
        pltpu.VMEM((ncols, SLOTS, CX), F32),
        pltpu.VMEM((ncols, SLOTS + 8, CX), F32),
        pltpu.SemaphoreType.DMA,
        pltpu.SemaphoreType.DMA((4,)),
        pltpu.SemaphoreType.DMA((4,)),
    ]
    payload = call(outgoing_kernel, [HBM, HBM], [(ncols, SLOTS + 8, CX)], scratch, HBM)(
        in_hbm(send_count.reshape(ncols)), in_hbm(partials.reshape(ncols, SLOTS, CX))
    )[0]
    incoming = lax.all_to_all(payload, "cols", split_axis=0, concat_axis=0, tiled=True)
    flat = (NZ * CY, CX)
    scratch = [
        pltpu.SMEM((NCLASS,), F32),
        pltpu.VMEM(flat, F32),
        pltpu.VMEM(flat, jnp.int32),
        pltpu.VMEM((ncols, SLOTS), jnp.int32),
        pltpu.SemaphoreType.DMA((4,)),
    ]
    fields = (class_cond, head_start.reshape(flat), class_map.reshape(flat), recv_block.reshape(ncols, SLOTS))
    head, cond, strip = call(fields_kernel, [HBM] * 4, [row, row, (CY // 2 + 1, 8, CX)], scratch)(
        *(in_hbm(x) for x in fields)
    )
    left = lax.ppermute(strip, "cols", forward(ncols))
    right = lax.ppermute(strip, "cols", backward(ncols))
    main, halo, up, down = call(recharge_kernel, [VMEM] * 6, [row, row, sent, sent])(
        incoming, strip, left, right, head, cond
    )
    top = lax.ppermute(down, "rows", forward(ngroups))
    bottom = lax.ppermute(up, "rows", backward(ngroups))
    place = jnp.stack([lax.axis_index("rows"), lax.axis_index("cols"), ngroups, ncols]).astype(jnp.int32)
    early = early_call(place, head, cond, main, halo, left, right)
    outs = late_call(0, place, top, early)
    return tuple(late_call(1, place, bottom, early, outs))


def solution(mesh):
    placed = (
        P(None, "rows", "cols"),
        P(None, "rows", "cols"),
        P(),
        P("rows", "cols", None, None, None),
        P("rows", "cols", None),
        P("rows", "cols", None, None),
    )
    return jax.shard_map(
        body,
        mesh=mesh,
        in_specs=placed,
        out_specs=(P(None, "rows", "cols"), P(None, "rows", "cols")),
        check_vma=False,
    )
```

```python
import functools

import jax
import jax.numpy as jnp
from jax import lax
from jax.experimental import pallas as pl
from jax.experimental.pallas import tpu as pltpu
from jax.sharding import PartitionSpec as P

NZ, CY, CX, SLOTS, NCLASS = 8, 32, 128, 32, 8
OMEGA = 0.8
NU1, NU2, NUC = 2, 2, 4
HY, HX = 14, 16
RY = 12
ROWS = CY + 2 * HY
LANES = 2 * CX
F32 = jnp.float32


def lane_of(shape):
    return lax.broadcasted_iota(jnp.int32, shape, len(shape) - 1)


def packed(rows, lane):
    out = None
    for q, row in enumerate(rows):
        turned = pltpu.roll(row, 32 * q + 16, 1)
        out = turned if q == 0 else jnp.where(lane // 32 == q, turned, out)
    return out


def unpacked(block, q, lane):
    turned = pltpu.roll(block, (CX - 32 * q - 16) % CX, 1)
    return jnp.where((lane < HX) | (lane >= CX - HX), turned, 0.0)


def outgoing_kernel(count_hbm, partials_hbm, out_hbm, count_ref, partials_ref, out_ref, count_sem, in_sems, out_sems):
    ncols = partials_ref.shape[0]
    part = ncols // 4
    counts = pltpu.make_async_copy(count_hbm, count_ref, count_sem)
    counts.start()
    arriving = []
    for c in range(4):
        piece = pl.ds(c * part, part)
        arriving.append(pltpu.make_async_copy(partials_hbm.at[piece], partials_ref.at[piece], in_sems.at[c]))
        arriving[c].start()
    counts.wait()
    lane = lane_of((8, CX))
    slot = lax.broadcasted_iota(jnp.int32, (8, CX), 0)
    zero = jnp.zeros((8, CX), F32)
    strips, leaving, sent = [zero], [], 0
    for d in range(ncols):
        if d % part == 0:
            arriving[d // part].wait()
        rows = []
        for q in range(SLOTS // 8):
            row = jnp.where(slot + 8 * q < count_ref[d], partials_ref[d, 8 * q : 8 * q + 8, :], 0.0)
            out_ref[d, 8 * q : 8 * q + 8, :] = row
            rows.append(row)
        strips.append(packed(rows, lane))
        if d == ncols - 1:
            strips.append(zero)
        ready = d + 1 if d == ncols - 1 else d
        for i in range(max(0, d - 1), ready):
            out_ref[i, SLOTS : SLOTS + 8, :] = jnp.where(lane % 32 < HX, strips[i], strips[i + 2])
        if d % part == part - 1:
            piece = pl.ds(sent, ready - sent)
            leaving.append(pltpu.make_async_copy(out_ref.at[piece], out_hbm.at[piece], out_sems.at[d // part]))
            leaving[-1].start()
            sent = ready
    for copy in leaving:
        copy.wait()


def fields_kernel(class_cond_hbm, head_hbm, class_hbm, ids_hbm, head_out, cond_out, right_out, left_out,
                  class_cond_ref, head_ref, class_ref, ids_ref, sems):
    pairs = (
        (head_hbm, head_ref), (class_hbm, class_ref), (class_cond_hbm, class_cond_ref), (ids_hbm, ids_ref)
    )
    copies = [pltpu.make_async_copy(a, b, sems.at[i]) for i, (a, b) in enumerate(pairs)]
    for copy in copies:
        copy.start()
    for copy in copies:
        copy.wait()
    lane = lane_of((8, CX))
    values = [class_cond_ref[c] for c in range(8)]
    blocks = []
    for block in range(CY // 4):
        heads, conds = [], []
        for q in range(4):
            y = 4 * block + q
            head = head_ref[pl.ds(y, NZ, stride=CY), :]
            kind = class_ref[pl.ds(y, NZ, stride=CY), :]
            cond = jnp.full((8, CX), values[0], F32)
            for c in range(1, 8):
                cond = jnp.where(kind == c, values[c], cond)
            head_out[y] = head
            cond_out[y] = cond
            heads.append(head)
            conds.append(cond)
        blocks.append((packed(heads, lane), packed(conds, lane)))
    near = lane % 32 < HX
    for f in range(2):
        for i in range(CY // 8):
            one, two = blocks[2 * i][f], blocks[2 * i + 1][f]
            right_out[f * (CY // 8) + i] = jnp.where(near, one, pltpu.roll(two, HX, 1))
            left_out[f * (CY // 8) + i] = jnp.where(near, pltpu.roll(one, CX - HX, 1), two)
    ids = ids_ref[...].astype(F32)
    count = ids.shape[0] // 4
    for out in (right_out, left_out):
        out[STRIP - 1] = jnp.zeros((8, CX), F32)
        for r in range(count):
            row = jnp.concatenate([ids[4 * r + q : 4 * r + q + 1, :] for q in range(4)], axis=1)
            out[STRIP - 1, r : r + 1, :] = row


STRIP = CY // 4 + 1


def four_rows(left_ref, right_ref, f, i, lane):
    left, right = left_ref[f * (CY // 8) + i // 2], right_ref[f * (CY // 8) + i // 2]
    if i % 2 == 0:
        return jnp.where(lane % 32 < HX, left, pltpu.roll(right, HX, 1))
    return jnp.where(lane % 32 < HX, pltpu.roll(left, CX - HX, 1), right)


def recharge_kernel(incoming_ref, own_ref, left_ref, right_ref, head_ref, cond_ref, main_out, halo_out, up_out, down_out):
    ncols = incoming_ref.shape[0]
    total = ncols * SLOTS
    chunk = min(256, total)
    senders = chunk // SLOTS
    lane = lane_of((8, CX))
    row = lax.broadcasted_iota(jnp.int32, (NZ * CY, chunk), 0)
    block_of = ((row % NZ) * CY + row // NZ).astype(F32)

    def onehot(ids, m):
        flat = jnp.concatenate([ids[r : r + 1, :] for r in range(m * chunk // CX, (m + 1) * chunk // CX)], axis=1)
        return jnp.where(block_of == flat, 1.0, 0.0).astype(jnp.bfloat16)

    def halves(values):
        high = values.astype(jnp.bfloat16)
        low = (values - high.astype(F32)).astype(jnp.bfloat16)
        return jnp.concatenate([high, low], axis=1)

    own, left, right = own_ref[STRIP - 1], left_ref[STRIP - 1], right_ref[STRIP - 1]
    main = jnp.zeros((NZ * CY, LANES), F32)
    from_left = jnp.zeros((NZ * CY, LANES), F32)
    from_right = jnp.zeros((NZ * CY, LANES), F32)
    for m in range(total // chunk):
        values = incoming_ref[m * senders : (m + 1) * senders, 0:SLOTS, :].reshape(chunk, CX)
        main = main + jnp.dot(onehot(own, m), halves(values), preferred_element_type=F32)
        strips = []
        for s in range(m * senders, (m + 1) * senders):
            strip = incoming_ref[s, SLOTS : SLOTS + 8, :]
            strips += [pltpu.roll(strip, (CX - 32 * q - 16) % CX, 1) for q in range(4)]
        edges = halves(jnp.concatenate(strips, axis=0))
        from_left = from_left + jnp.dot(onehot(left, m), edges, preferred_element_type=F32)
        from_right = from_right + jnp.dot(onehot(right, m), edges, preferred_element_type=F32)
    main = (main[:, :CX] + main[:, CX:]).reshape(CY, NZ, CX)
    from_left = (from_left[:, :CX] + from_left[:, CX:]).reshape(CY, NZ, CX)
    from_right = (from_right[:, :CX] + from_right[:, CX:]).reshape(CY, NZ, CX)
    wide = lane_of((CY, NZ, CX))
    halo = jnp.where(wide >= CX - HX, from_left, jnp.where(wide < HX, from_right, 0.0))
    main_out[...] = main
    halo_out[...] = halo
    for out, first, strip0 in ((up_out, 0, 0), (down_out, CY - HY, CY // 4 - 4)):
        skip = first and HY - RY
        out[0:HY] = head_ref[first : first + HY]
        out[HY : 2 * HY] = cond_ref[first : first + HY]
        out[2 * HY : 2 * HY + RY] = main[first + skip : first + skip + RY]
        base = 2 * HY + RY
        for i in range(4):
            for f in range(2):
                out[base + 4 * f + i] = four_rows(left_ref, right_ref, f, strip0 + i, lane)
        for i in range(RY // 4):
            y = first + skip + 4 * i
            out[base + 8 + i] = packed([halo[y + q] for q in range(4)], lane)


SENT = 2 * HY + RY + 8 + RY // 4


def span(first, last):
    return list(range(first, last + 1))


NEEDED = {
    "u0": (span(1, 58), span(14, 45)),
    "half": (span(1, 58), span(14, 45)),
    "source": (span(2, 57), span(14, 45)),
    "fx": (span(2, 57), span(14, 45)),
    "fy": (span(1, 57), span(14, 44)),
    "fz": (span(2, 57), span(14, 45)),
    "weight": (span(2, 57), span(15, 44)),
    "u1": (span(2, 57), span(15, 44)),
    "u2": (span(3, 56), span(16, 43)),
    "c_half": (span(1, 28), span(7, 22)),
    "c_fx": (span(2, 27), span(7, 22)),
    "c_fy": (span(1, 27), span(7, 21)),
    "c_fz": (span(2, 27), span(7, 22)),
    "c_weight": (span(2, 27), span(8, 21)),
    "c_source": (span(2, 27), span(9, 20)),
    "c_u0": (span(2, 27), span(9, 20)),
    "c_u1": (span(3, 26), span(10, 19)),
    "c_u2": (span(4, 25), span(11, 18)),
    "c_u3": (span(5, 24), span(12, 17)),
    "u3": (span(11, 48), span(24, 35)),
    "u4": (span(12, 47), span(25, 34)),
    "u5": (span(13, 46), span(26, 33)),
    "residual": (span(14, 45), span(27, 32)),
}
EARLY, LATE = {}, ({}, {})
for _name, (_every, _own) in NEEDED.items():
    for _r in _every:
        _into = EARLY if _r in _own else LATE[0 if _r < _own[0] else 1]
        _into[_name, _r] = len(_into)


class Cycle:
    def __init__(self, place_ref, early, late=None, side=None):
        self.early, self.late, self.side = early, late, side
        self.lane = lane_of((1, NZ, LANES))
        layer = lax.broadcasted_iota(jnp.int32, (1, NZ, LANES), 1)
        self.below = jnp.where(layer < NZ - 1, 1.0, 0.0)
        self.even = self.lane % 2 == 0
        g, d, ngroups, ncols = place_ref[0], place_ref[1], place_ref[2], place_ref[3]
        right = jnp.where(d < ncols - 1, CX + HX, CX)
        left = jnp.where(d > 0, LANES - HX, LANES)
        columns = jnp.where((self.lane < right) | (self.lane >= left), OMEGA, 0.0)
        above, under = jnp.where(g > 0, 1.0, 0.0), jnp.where(g < ngroups - 1, 1.0, 0.0)
        self.inside = (columns * above, columns, columns * under)

    def ranges(self, name):
        every, own = NEEDED[name]
        if self.late is None:
            return [(own[0], len(own), 1)]
        if self.side == 0:
            return [(every[0], own[0] - every[0], 0)]
        return [(own[-1] + 1, every[-1] - own[-1], 2)]

    def get(self, name, r, n):
        parts, at = [], r
        while at < r + n:
            ref, rows = (self.early, EARLY) if (name, at) in EARLY else (self.late, LATE[self.side])
            many = 1
            while at + many < r + n and rows.get((name, at + many)) == rows[name, at] + many:
                many += 1
            parts.append(ref[pl.ds(rows[name, at], many)])
            at += many
        return parts[0] if len(parts) == 1 else jnp.concatenate(parts, axis=0)

    def put(self, name, r, n, value):
        if self.late is None:
            self.early[pl.ds(EARLY[name, r], n)] = value
        else:
            self.late[pl.ds(LATE[self.side][name, r], n)] = value

    def put_parts(self, name, r, main, halo):
        ref, at = (self.early, EARLY[name, r]) if self.late is None else (self.late, LATE[self.side][name, r])
        ref[at, :, 0:CX] = main
        ref[at, :, CX:LANES] = halo

    def turn(self, x, by):
        return pltpu.roll(x, by % LANES, 2)

    def turn_z(self, x, by):
        return pltpu.roll(x, by % NZ, 1)

    def pairs(self, x):
        two = x.reshape(x.shape[0] // 2, 2, NZ, LANES)
        two = two[:, 0] + two[:, 1]
        return two + jnp.where(self.even, self.turn(two, -1), self.turn(two, 1))

    def coefficients(self, mark, shift, zweight, own):
        for r, n, _ in self.ranges(mark + "fx"):
            k = self.get(mark + "half", r, n)
            self.put(mark + "fx", r, n, k + self.turn(k, -shift))
            self.put(mark + "fz", r, n, (k + self.turn_z(k, -1)) * (zweight * self.below))
        for r, n, _ in self.ranges(mark + "fy"):
            k = self.get(mark + "half", r, n + 1)
            self.put(mark + "fy", r, n, k[:-1] + k[1:])
        for r, n, part in self.ranges(mark + "weight"):
            pieces = [(r, n, part)]
            if part == 0:
                pieces = [(r, own[0] - r, 0), (own[0], r + n - own[0], 1)]
            elif part == 2:
                pieces = [(r, own[1] + 1 - r, 1), (own[1] + 1, r + n - own[1] - 1, 2)]
            for at, many, which in pieces:
                x, z = self.get(mark + "fx", at, many), self.get(mark + "fz", at, many)
                y = self.get(mark + "fy", at - 1, many + 1)
                total = (x + self.turn(x, shift)) + (y[1:] + y[:-1]) + (z + self.turn_z(z, 1))
                scale = self.inside[which]
                self.put(mark + "weight", at, many, scale / jnp.where(scale > 0.0, total, 1.0))

    def operator(self, u, mark, shift, r, n):
        v = self.get(u, r - 1, n + 2)
        own = v[1:-1]
        x = self.get(mark + "fx", r, n) * (own - self.turn(own, -shift))
        y = self.get(mark + "fy", r - 1, n + 1) * (v[:-1] - v[1:])
        z = self.get(mark + "fz", r, n) * (self.turn_z(own, -1) - own)
        return own, (x - self.turn(x, shift)) + (y[1:] - y[:-1]) + (z - self.turn_z(z, 1))

    def sweep(self, old, new, mark, shift):
        for r, n, _ in self.ranges(new):
            own, applied = self.operator(old, mark, shift, r, n)
            left = self.get(mark + "source", r, n) - applied
            self.put(new, r, n, own + self.get(mark + "weight", r, n) * left)

    def run(self, done):
        self.coefficients("", 1, 1.0, (HY, HY + CY - 1))
        self.sweep("u0", "u1", "", 1)
        self.sweep("u1", "u2", "", 1)
        for c, n, _ in self.ranges("c_half"):
            self.put("c_half", c, n, 0.25 * self.pairs(self.get("half", 2 * c, 2 * n)))
        self.coefficients("c_", 2, 4.0, (HY // 2, HY // 2 + CY // 2 - 1))
        for c, n, _ in self.ranges("c_source"):
            _, applied = self.operator("u2", "", 1, 2 * c, 2 * n)
            summed = self.pairs(self.get("source", 2 * c, 2 * n) - applied)
            self.put("c_source", c, n, summed)
            self.put("c_u0", c, n, self.get("c_weight", c, n) * summed)
        for i in range(1, NUC):
            self.sweep("c_u%d" % (i - 1), "c_u%d" % i, "c_", 2)
        for r, n, _ in self.ranges("u3"):
            c, many = r // 2, (r + n - 1) // 2 - r // 2 + 1
            added = self.get("c_u%d" % (NUC - 1), c, many)
            added = jnp.broadcast_to(added[:, None], (many, 2, NZ, LANES)).reshape(2 * many, NZ, LANES)
            self.put("u3", r, n, self.get("u2", r, n) + added[r % 2 : r % 2 + n])
        self.sweep("u3", "u4", "", 1)
        self.sweep("u4", "u5", "", 1)
        done()
        for r, n, _ in self.ranges("residual"):
            _, applied = self.operator("u5", "", 1, r, n)
            self.put("residual", r, n, self.get("source", r, n) - applied)


def early_kernel(place_ref, head_ref, cond_ref, main_ref, halo_ref, left_ref, right_ref, early):
    cycle = Cycle(place_ref, early)
    lane = lane_of((8, CX))
    for i in range(CY // 4):
        heads = four_rows(left_ref, right_ref, 0, i, lane)
        conds = 0.5 * four_rows(left_ref, right_ref, 1, i, lane)
        for q in range(4):
            y = 4 * i + q
            cycle.put_parts("u0", HY + y, head_ref[y], unpacked(heads, q, lane))
            cycle.put_parts("half", HY + y, 0.5 * cond_ref[y], unpacked(conds, q, lane))
            cycle.put_parts("source", HY + y, main_ref[y], halo_ref[y])
    cycle.run(lambda: None)


def late_kernel(side, place_ref, sent_ref, early, *refs):
    copies = []
    if side == 0:
        head_ref, residual_ref, late = refs
    else:
        upper_head, upper_residual, head_hbm, residual_hbm, late, head_ref, residual_ref, sems = refs
        top, bottom = pl.ds(0, CY // 2), pl.ds(CY // 2, CY // 2)
        pairs = (
            (upper_head, head_hbm.at[:, top, :]), (upper_residual, residual_hbm.at[:, top, :]),
            (head_ref, head_hbm.at[:, bottom, :]), (residual_ref, residual_hbm.at[:, bottom, :]),
        )
        copies = [pltpu.make_async_copy(a, b, sems.at[i]) for i, (a, b) in enumerate(pairs)]
        copies[0].start()
        copies[1].start()
    cycle = Cycle(place_ref, early, late, side)
    lane = lane_of((8, CX))
    base = 2 * HY + RY
    first, shift, skip = ((0, 2, HY - RY), (HY + CY, 0, 0))[side]
    for i in range(HY):
        at, q = (i + shift) // 4, (i + shift) % 4
        if first + i in NEEDED["u0"][0]:
            cycle.put_parts("u0", first + i, sent_ref[i], unpacked(sent_ref[base + at], q, lane))
            half = 0.5 * sent_ref[HY + i]
            cycle.put_parts("half", first + i, half, 0.5 * unpacked(sent_ref[base + 4 + at], q, lane))
    for i in range(RY):
        edge = unpacked(sent_ref[base + 8 + i // 4], i % 4, lane)
        cycle.put_parts("source", first + skip + i, sent_ref[2 * HY + i], edge)
    def leave(name, ref):
        for y in range(CY // 2):
            ref[:, y, :] = cycle.get(name, HY + side * (CY // 2) + y, 1)[0, :, 0:CX]

    def head_done():
        leave("u5", head_ref)
        for copy in copies[2:3]:
            copy.start()

    cycle.run(head_done)
    leave("residual", residual_ref)
    for copy in copies[3:]:
        copy.start()
    for copy in copies:
        copy.wait()


VMEM = pl.BlockSpec(memory_space=pltpu.VMEM)
SMEM = pl.BlockSpec(memory_space=pltpu.SMEM)
HBM = pl.BlockSpec(memory_space=pltpu.HBM)


def in_hbm(x):
    return pltpu.with_memory_space_constraint(x, pltpu.HBM)


def call(kernel, ins, outs, scratch=(), out=VMEM, flops=1 << 20, nbytes=1 << 20):
    return pl.pallas_call(
        kernel,
        out_shape=tuple(jax.ShapeDtypeStruct(s, F32) for s in outs),
        in_specs=ins,
        out_specs=tuple(out for _ in outs),
        scratch_shapes=scratch,
        cost_estimate=pl.CostEstimate(flops=flops, bytes_accessed=nbytes, transcendentals=0),
        compiler_params=pltpu.CompilerParams(vmem_limit_bytes=32 << 20),
    )


def forward(count):
    return [(i, i + 1) for i in range(count - 1)]


def backward(count):
    return [(i + 1, i) for i in range(count - 1)]


def early_call(place, head, cond, main, halo, left, right):
    return call(early_kernel, [SMEM] + [VMEM] * 6, [(len(EARLY), NZ, LANES)])(
        place, head, cond, main, halo, left, right
    )[0]


def late_call(side, place, sent, early, upper=()):
    half = (NZ, CY // 2, CX)
    late = pltpu.VMEM((len(LATE[side]), NZ, LANES), F32)
    kernel, ins = functools.partial(late_kernel, side), [SMEM] + [VMEM] * (2 + len(upper))
    if side == 0:
        return call(kernel, ins, [half] * 2, [late])(place, sent, early)
    scratch = [late] + [pltpu.VMEM(half, F32)] * 2 + [pltpu.SemaphoreType.DMA((4,))]
    return call(kernel, ins, [(NZ, CY, CX)] * 2, scratch, HBM)(place, sent, early, *upper)


def body(head_start, class_map, class_cond, partials, send_count, recv_block):
    ngroups, ncols = lax.axis_size("rows"), lax.axis_size("cols")
    row, sent = (CY, NZ, CX), (SENT, 8, CX)
    scratch = [
        pltpu.SMEM((ncols,), jnp.int32),
        pltpu.VMEM((ncols, SLOTS, CX), F32),
        pltpu.VMEM((ncols, SLOTS + 8, CX), F32),
        pltpu.SemaphoreType.DMA,
        pltpu.SemaphoreType.DMA((4,)),
        pltpu.SemaphoreType.DMA((4,)),
    ]
    payload = call(outgoing_kernel, [HBM, HBM], [(ncols, SLOTS + 8, CX)], scratch, HBM)(
        in_hbm(send_count.reshape(ncols)), in_hbm(partials.reshape(ncols, SLOTS, CX))
    )[0]
    incoming = lax.all_to_all(payload, "cols", split_axis=0, concat_axis=0, tiled=True)
    flat = (NZ * CY, CX)
    scratch = [
        pltpu.SMEM((NCLASS,), F32),
        pltpu.VMEM(flat, F32),
        pltpu.VMEM(flat, jnp.int32),
        pltpu.VMEM((ncols, SLOTS), jnp.int32),
        pltpu.SemaphoreType.DMA((4,)),
    ]
    fields = (class_cond, head_start.reshape(flat), class_map.reshape(flat), recv_block.reshape(ncols, SLOTS))
    head, cond, to_right, to_left = call(fields_kernel, [HBM] * 4, [row, row] + [(STRIP, 8, CX)] * 2, scratch)(
        *(in_hbm(x) for x in fields)
    )
    left = lax.ppermute(to_right, "cols", forward(ncols))
    right = lax.ppermute(to_left, "cols", backward(ncols))
    main, halo, up, down = call(recharge_kernel, [VMEM] * 6, [row, row, sent, sent])(
        incoming, to_right, left, right, head, cond
    )
    top = lax.ppermute(down, "rows", forward(ngroups))
    bottom = lax.ppermute(up, "rows", backward(ngroups))
    place = jnp.stack([lax.axis_index("rows"), lax.axis_index("cols"), ngroups, ncols]).astype(jnp.int32)
    early = early_call(place, head, cond, main, halo, left, right)
    upper = late_call(0, place, top, early)
    return tuple(late_call(1, place, bottom, early, upper))


def solution(mesh):
    placed = (
        P(None, "rows", "cols"),
        P(None, "rows", "cols"),
        P(),
        P("rows", "cols", None, None, None),
        P("rows", "cols", None),
        P("rows", "cols", None, None),
    )
    return jax.shard_map(
        body,
        mesh=mesh,
        in_specs=placed,
        out_specs=(P(None, "rows", "cols"), P(None, "rows", "cols")),
        check_vma=False,
    )
```

```python
import functools

import jax
import jax.numpy as jnp
from jax import lax
from jax.experimental import pallas as pl
from jax.experimental.pallas import tpu as pltpu
from jax.sharding import PartitionSpec as P

NZ, CY, CX, SLOTS, NCLASS = 8, 32, 128, 32, 8
OMEGA = 0.8
NU1, NU2, NUC = 2, 2, 4
HY, HX = 14, 16
RY = 12
ROWS = CY + 2 * HY
LANES = 2 * CX
F32 = jnp.float32


def lane_of(shape):
    return lax.broadcasted_iota(jnp.int32, shape, len(shape) - 1)


def packed(rows, lane):
    out = None
    for q, row in enumerate(rows):
        turned = pltpu.roll(row, 32 * q + 16, 1)
        out = turned if q == 0 else jnp.where(lane // 32 == q, turned, out)
    return out


def unpacked(block, q, lane):
    turned = pltpu.roll(block, (CX - 32 * q - 16) % CX, 1)
    return jnp.where((lane < HX) | (lane >= CX - HX), turned, 0.0)


def outgoing_kernel(count_hbm, partials_hbm, out_hbm, count_ref, partials_ref, out_ref, count_sem, in_sems, out_sems):
    ncols = partials_ref.shape[0]
    part = ncols // 4
    counts = pltpu.make_async_copy(count_hbm, count_ref, count_sem)
    counts.start()
    arriving = []
    for c in range(4):
        piece = pl.ds(c * part, part)
        arriving.append(pltpu.make_async_copy(partials_hbm.at[piece], partials_ref.at[piece], in_sems.at[c]))
        arriving[c].start()
    counts.wait()
    lane = lane_of((8, CX))
    slot = lax.broadcasted_iota(jnp.int32, (8, CX), 0)
    zero = jnp.zeros((8, CX), F32)
    strips, leaving, sent = [zero], [], 0
    for d in range(ncols):
        if d % part == 0:
            arriving[d // part].wait()
        rows = []
        for q in range(SLOTS // 8):
            row = jnp.where(slot + 8 * q < count_ref[d], partials_ref[d, 8 * q : 8 * q + 8, :], 0.0)
            out_ref[d, 8 * q : 8 * q + 8, :] = row
            rows.append(row)
        strips.append(packed(rows, lane))
        if d == ncols - 1:
            strips.append(zero)
        ready = d + 1 if d == ncols - 1 else d
        for i in range(max(0, d - 1), ready):
            out_ref[i, SLOTS : SLOTS + 8, :] = jnp.where(lane % 32 < HX, strips[i], strips[i + 2])
        if d % part == part - 1:
            piece = pl.ds(sent, ready - sent)
            leaving.append(pltpu.make_async_copy(out_ref.at[piece], out_hbm.at[piece], out_sems.at[d // part]))
            leaving[-1].start()
            sent = ready
    for copy in leaving:
        copy.wait()


def fields_kernel(class_cond_hbm, head_hbm, class_hbm, ids_hbm, head_out, cond_out, right_out, left_out, edge_out,
                  class_cond_ref, head_ref, class_ref, ids_ref, sems):
    pairs = (
        (head_hbm, head_ref), (class_hbm, class_ref), (class_cond_hbm, class_cond_ref), (ids_hbm, ids_ref)
    )
    copies = [pltpu.make_async_copy(a, b, sems.at[i]) for i, (a, b) in enumerate(pairs)]
    for copy in copies:
        copy.start()
    for copy in copies:
        copy.wait()
    lane = lane_of((8, CX))
    values = [class_cond_ref[c] for c in range(8)]
    blocks = []
    for block in range(CY // 4):
        heads, conds = [], []
        for q in range(4):
            y = 4 * block + q
            head = head_ref[pl.ds(y, NZ, stride=CY), :]
            kind = class_ref[pl.ds(y, NZ, stride=CY), :]
            cond = jnp.full((8, CX), values[0], F32)
            for c in range(1, 8):
                cond = jnp.where(kind == c, values[c], cond)
            head_out[y] = head
            cond_out[y] = cond
            if y < HY:
                edge_out[y] = head
                edge_out[HY + y] = cond
            heads.append(head)
            conds.append(cond)
        blocks.append((packed(heads, lane), packed(conds, lane)))
    near = lane % 32 < HX
    for f in range(2):
        for i in range(CY // 8):
            one, two = blocks[2 * i][f], blocks[2 * i + 1][f]
            right_out[f * (CY // 8) + i] = jnp.where(near, one, pltpu.roll(two, HX, 1))
            left_out[f * (CY // 8) + i] = jnp.where(near, pltpu.roll(one, CX - HX, 1), two)
    ids = ids_ref[...].astype(F32)
    count = ids.shape[0] // 4
    for out in (right_out, left_out):
        out[STRIP - 1] = jnp.zeros((8, CX), F32)
        for r in range(count):
            row = jnp.concatenate([ids[4 * r + q : 4 * r + q + 1, :] for q in range(4)], axis=1)
            out[STRIP - 1, r : r + 1, :] = row


STRIP = CY // 4 + 1


def four_rows(left_ref, right_ref, f, i, lane):
    left, right = left_ref[f * (CY // 8) + i // 2], right_ref[f * (CY // 8) + i // 2]
    if i % 2 == 0:
        return jnp.where(lane % 32 < HX, left, pltpu.roll(right, HX, 1))
    return jnp.where(lane % 32 < HX, pltpu.roll(left, CX - HX, 1), right)


def recharge_kernel(incoming_ref, own_ref, left_ref, right_ref, head_ref, cond_ref, _,
                    main_out, halo_out, up_out, down_out):
    ncols = incoming_ref.shape[0]
    total = ncols * SLOTS
    chunk = min(256, total)
    senders = chunk // SLOTS
    lane = lane_of((8, CX))
    row = lax.broadcasted_iota(jnp.int32, (NZ * CY, chunk), 0)
    block_of = ((row % NZ) * CY + row // NZ).astype(F32)

    def onehot(ids, m):
        flat = jnp.concatenate([ids[r : r + 1, :] for r in range(m * chunk // CX, (m + 1) * chunk // CX)], axis=1)
        return jnp.where(block_of == flat, 1.0, 0.0).astype(jnp.bfloat16)

    def halves(values):
        high = values.astype(jnp.bfloat16)
        low = (values - high.astype(F32)).astype(jnp.bfloat16)
        return jnp.concatenate([high, low], axis=1)

    own, left, right = own_ref[STRIP - 1], left_ref[STRIP - 1], right_ref[STRIP - 1]
    main = jnp.zeros((NZ * CY, LANES), F32)
    from_left = jnp.zeros((NZ * CY, LANES), F32)
    from_right = jnp.zeros((NZ * CY, LANES), F32)
    for m in range(total // chunk):
        values = incoming_ref[m * senders : (m + 1) * senders, 0:SLOTS, :].reshape(chunk, CX)
        main = main + jnp.dot(onehot(own, m), halves(values), preferred_element_type=F32)
        strips = []
        for s in range(m * senders, (m + 1) * senders):
            strip = incoming_ref[s, SLOTS : SLOTS + 8, :]
            strips += [pltpu.roll(strip, (CX - 32 * q - 16) % CX, 1) for q in range(4)]
        edges = halves(jnp.concatenate(strips, axis=0))
        from_left = from_left + jnp.dot(onehot(left, m), edges, preferred_element_type=F32)
        from_right = from_right + jnp.dot(onehot(right, m), edges, preferred_element_type=F32)
    main = (main[:, :CX] + main[:, CX:]).reshape(CY, NZ, CX)
    from_left = (from_left[:, :CX] + from_left[:, CX:]).reshape(CY, NZ, CX)
    from_right = (from_right[:, :CX] + from_right[:, CX:]).reshape(CY, NZ, CX)
    wide = lane_of((CY, NZ, CX))
    halo = jnp.where(wide >= CX - HX, from_left, jnp.where(wide < HX, from_right, 0.0))
    main_out[...] = main
    halo_out[...] = halo
    for out, first, strip0, base in ((up_out, 0, 0, 0), (down_out, CY - HY, CY // 4 - 4, 2 * HY)):
        skip = first and HY - RY
        if base:
            out[0:HY] = head_ref[first : first + HY]
            out[HY : 2 * HY] = cond_ref[first : first + HY]
        out[base : base + RY] = main[first + skip : first + skip + RY]
        base = base + RY
        for i in range(4):
            for f in range(2):
                out[base + 4 * f + i] = four_rows(left_ref, right_ref, f, strip0 + i, lane)
        for i in range(RY // 4):
            y = first + skip + 4 * i
            out[base + 8 + i] = packed([halo[y + q] for q in range(4)], lane)


EDGE, UP = 2 * HY, RY + 8 + RY // 4
DOWN = EDGE + UP


def span(first, last):
    return list(range(first, last + 1))


NEEDED = {
    "u0": (span(1, 58), span(14, 45)),
    "half": (span(1, 58), span(14, 45)),
    "source": (span(2, 57), span(14, 45)),
    "fx": (span(2, 57), span(14, 45)),
    "fy": (span(1, 57), span(14, 44)),
    "fz": (span(2, 57), span(14, 45)),
    "weight": (span(2, 57), span(15, 44)),
    "u1": (span(2, 57), span(15, 44)),
    "u2": (span(3, 56), span(16, 43)),
    "c_half": (span(1, 28), span(7, 22)),
    "c_fx": (span(2, 27), span(7, 22)),
    "c_fy": (span(1, 27), span(7, 21)),
    "c_fz": (span(2, 27), span(7, 22)),
    "c_weight": (span(2, 27), span(8, 21)),
    "c_source": (span(2, 27), span(9, 20)),
    "c_u0": (span(2, 27), span(9, 20)),
    "c_u1": (span(3, 26), span(10, 19)),
    "c_u2": (span(4, 25), span(11, 18)),
    "c_u3": (span(5, 24), span(12, 17)),
    "u3": (span(11, 48), span(24, 35)),
    "u4": (span(12, 47), span(25, 34)),
    "u5": (span(13, 46), span(26, 33)),
    "residual": (span(14, 45), span(27, 32)),
}
EARLY, LATE = {}, ({}, {})
for _name, (_every, _own) in NEEDED.items():
    for _r in _every:
        _into = EARLY if _r in _own else LATE[0 if _r < _own[0] else 1]
        _into[_name, _r] = len(_into)


class Cycle:
    def __init__(self, place_ref, early, late=None, side=None):
        self.early, self.late, self.side = early, late, side
        self.lane = lane_of((1, NZ, LANES))
        layer = lax.broadcasted_iota(jnp.int32, (1, NZ, LANES), 1)
        self.below = jnp.where(layer < NZ - 1, 1.0, 0.0)
        self.even = self.lane % 2 == 0
        g, d, ngroups, ncols = place_ref[0], place_ref[1], place_ref[2], place_ref[3]
        right = jnp.where(d < ncols - 1, CX + HX, CX)
        left = jnp.where(d > 0, LANES - HX, LANES)
        columns = jnp.where((self.lane < right) | (self.lane >= left), OMEGA, 0.0)
        above, under = jnp.where(g > 0, 1.0, 0.0), jnp.where(g < ngroups - 1, 1.0, 0.0)
        self.inside = (columns * above, columns, columns * under)

    def ranges(self, name):
        every, own = NEEDED[name]
        if self.late is None:
            return [(own[0], len(own), 1)]
        if self.side == 0:
            return [(every[0], own[0] - every[0], 0)]
        return [(own[-1] + 1, every[-1] - own[-1], 2)]

    def get(self, name, r, n):
        parts, at = [], r
        while at < r + n:
            ref, rows = (self.early, EARLY) if (name, at) in EARLY else (self.late, LATE[self.side])
            many = 1
            while at + many < r + n and rows.get((name, at + many)) == rows[name, at] + many:
                many += 1
            parts.append(ref[pl.ds(rows[name, at], many)])
            at += many
        return parts[0] if len(parts) == 1 else jnp.concatenate(parts, axis=0)

    def put(self, name, r, n, value):
        if self.late is None:
            self.early[pl.ds(EARLY[name, r], n)] = value
        else:
            self.late[pl.ds(LATE[self.side][name, r], n)] = value

    def put_parts(self, name, r, main, halo):
        ref, at = (self.early, EARLY[name, r]) if self.late is None else (self.late, LATE[self.side][name, r])
        ref[at, :, 0:CX] = main
        ref[at, :, CX:LANES] = halo

    def turn(self, x, by):
        return pltpu.roll(x, by % LANES, 2)

    def turn_z(self, x, by):
        return pltpu.roll(x, by % NZ, 1)

    def pairs(self, x):
        two = x.reshape(x.shape[0] // 2, 2, NZ, LANES)
        two = two[:, 0] + two[:, 1]
        return two + jnp.where(self.even, self.turn(two, -1), self.turn(two, 1))

    def coefficients(self, mark, shift, zweight, own):
        for r, n, _ in self.ranges(mark + "fx"):
            k = self.get(mark + "half", r, n)
            self.put(mark + "fx", r, n, k + self.turn(k, -shift))
            self.put(mark + "fz", r, n, (k + self.turn_z(k, -1)) * (zweight * self.below))
        for r, n, _ in self.ranges(mark + "fy"):
            k = self.get(mark + "half", r, n + 1)
            self.put(mark + "fy", r, n, k[:-1] + k[1:])
        for r, n, part in self.ranges(mark + "weight"):
            pieces = [(r, n, part)]
            if part == 0:
                pieces = [(r, own[0] - r, 0), (own[0], r + n - own[0], 1)]
            elif part == 2:
                pieces = [(r, own[1] + 1 - r, 1), (own[1] + 1, r + n - own[1] - 1, 2)]
            for at, many, which in pieces:
                x, z = self.get(mark + "fx", at, many), self.get(mark + "fz", at, many)
                y = self.get(mark + "fy", at - 1, many + 1)
                total = (x + self.turn(x, shift)) + (y[1:] + y[:-1]) + (z + self.turn_z(z, 1))
                scale = self.inside[which]
                self.put(mark + "weight", at, many, scale / jnp.where(scale > 0.0, total, 1.0))

    def operator(self, u, mark, shift, r, n):
        v = self.get(u, r - 1, n + 2)
        own = v[1:-1]
        x = self.get(mark + "fx", r, n) * (own - self.turn(own, -shift))
        y = self.get(mark + "fy", r - 1, n + 1) * (v[:-1] - v[1:])
        z = self.get(mark + "fz", r, n) * (self.turn_z(own, -1) - own)
        return own, (x - self.turn(x, shift)) + (y[1:] - y[:-1]) + (z - self.turn_z(z, 1))

    def sweep(self, old, new, mark, shift):
        for r, n, _ in self.ranges(new):
            own, applied = self.operator(old, mark, shift, r, n)
            left = self.get(mark + "source", r, n) - applied
            self.put(new, r, n, own + self.get(mark + "weight", r, n) * left)

    def run(self, done):
        self.coefficients("", 1, 1.0, (HY, HY + CY - 1))
        self.sweep("u0", "u1", "", 1)
        self.sweep("u1", "u2", "", 1)
        for c, n, _ in self.ranges("c_half"):
            self.put("c_half", c, n, 0.25 * self.pairs(self.get("half", 2 * c, 2 * n)))
        self.coefficients("c_", 2, 4.0, (HY // 2, HY // 2 + CY // 2 - 1))
        for c, n, _ in self.ranges("c_source"):
            _, applied = self.operator("u2", "", 1, 2 * c, 2 * n)
            summed = self.pairs(self.get("source", 2 * c, 2 * n) - applied)
            self.put("c_source", c, n, summed)
            self.put("c_u0", c, n, self.get("c_weight", c, n) * summed)
        for i in range(1, NUC):
            self.sweep("c_u%d" % (i - 1), "c_u%d" % i, "c_", 2)
        for r, n, _ in self.ranges("u3"):
            c, many = r // 2, (r + n - 1) // 2 - r // 2 + 1
            added = self.get("c_u%d" % (NUC - 1), c, many)
            added = jnp.broadcast_to(added[:, None], (many, 2, NZ, LANES)).reshape(2 * many, NZ, LANES)
            self.put("u3", r, n, self.get("u2", r, n) + added[r % 2 : r % 2 + n])
        self.sweep("u3", "u4", "", 1)
        self.sweep("u4", "u5", "", 1)
        done()
        for r, n, _ in self.ranges("residual"):
            _, applied = self.operator("u5", "", 1, r, n)
            self.put("residual", r, n, self.get("source", r, n) - applied)


def early_kernel(place_ref, head_ref, cond_ref, main_ref, halo_ref, left_ref, right_ref, early):
    cycle = Cycle(place_ref, early)
    lane = lane_of((8, CX))
    for i in range(CY // 4):
        heads = four_rows(left_ref, right_ref, 0, i, lane)
        conds = 0.5 * four_rows(left_ref, right_ref, 1, i, lane)
        for q in range(4):
            y = 4 * i + q
            cycle.put_parts("u0", HY + y, head_ref[y], unpacked(heads, q, lane))
            cycle.put_parts("half", HY + y, 0.5 * cond_ref[y], unpacked(conds, q, lane))
            cycle.put_parts("source", HY + y, main_ref[y], halo_ref[y])
    cycle.run(lambda: None)


def late_kernel(side, place_ref, sent_ref, early, *refs):
    copies = []
    if side == 0:
        head_ref, residual_ref, late = refs
        edge_ref = sent_ref
    else:
        edge_ref, upper_head, upper_residual, head_hbm, residual_hbm, late, head_ref, residual_ref, sems = refs
        top, bottom = pl.ds(0, CY // 2), pl.ds(CY // 2, CY // 2)
        pairs = (
            (upper_head, head_hbm.at[:, top, :]), (upper_residual, residual_hbm.at[:, top, :]),
            (head_ref, head_hbm.at[:, bottom, :]), (residual_ref, residual_hbm.at[:, bottom, :]),
        )
        copies = [pltpu.make_async_copy(a, b, sems.at[i]) for i, (a, b) in enumerate(pairs)]
        copies[0].start()
        copies[1].start()
    cycle = Cycle(place_ref, early, late, side)
    lane = lane_of((8, CX))
    base, source = (EDGE + RY, EDGE) if side == 0 else (RY, 0)
    first, shift, skip = ((0, 2, HY - RY), (HY + CY, 0, 0))[side]
    for i in range(HY):
        at, q = (i + shift) // 4, (i + shift) % 4
        if first + i in NEEDED["u0"][0]:
            cycle.put_parts("u0", first + i, edge_ref[i], unpacked(sent_ref[base + at], q, lane))
            half = 0.5 * edge_ref[HY + i]
            cycle.put_parts("half", first + i, half, 0.5 * unpacked(sent_ref[base + 4 + at], q, lane))
    for i in range(RY):
        edge = unpacked(sent_ref[base + 8 + i // 4], i % 4, lane)
        cycle.put_parts("source", first + skip + i, sent_ref[source + i], edge)

    def leave(name, ref):
        for y in range(CY // 2):
            ref[:, y, :] = cycle.get(name, HY + side * (CY // 2) + y, 1)[0, :, 0:CX]

    def head_done():
        leave("u5", head_ref)
        for copy in copies[2:3]:
            copy.start()

    cycle.run(head_done)
    leave("residual", residual_ref)
    for copy in copies[3:]:
        copy.start()
    for copy in copies:
        copy.wait()


VMEM = pl.BlockSpec(memory_space=pltpu.VMEM)
SMEM = pl.BlockSpec(memory_space=pltpu.SMEM)
HBM = pl.BlockSpec(memory_space=pltpu.HBM)
ANY = pl.BlockSpec(memory_space=pl.ANY)


def in_hbm(x):
    return pltpu.with_memory_space_constraint(x, pltpu.HBM)


def call(kernel, ins, outs, scratch=(), out=VMEM, flops=1 << 20, nbytes=1 << 20):
    return pl.pallas_call(
        kernel,
        out_shape=tuple(jax.ShapeDtypeStruct(s, F32) for s in outs),
        in_specs=ins,
        out_specs=tuple(out for _ in outs),
        scratch_shapes=scratch,
        cost_estimate=pl.CostEstimate(flops=flops, bytes_accessed=nbytes, transcendentals=0),
        compiler_params=pltpu.CompilerParams(vmem_limit_bytes=32 << 20),
    )


def forward(count):
    return [(i, i + 1) for i in range(count - 1)]


def backward(count):
    return [(i + 1, i) for i in range(count - 1)]


def early_call(place, head, cond, main, halo, left, right):
    return call(early_kernel, [SMEM] + [VMEM] * 6, [(len(EARLY), NZ, LANES)])(
        place, head, cond, main, halo, left, right
    )[0]


def late_call(side, place, sent, early, others=()):
    half = (NZ, CY // 2, CX)
    late = pltpu.VMEM((len(LATE[side]), NZ, LANES), F32)
    kernel, ins = functools.partial(late_kernel, side), [SMEM] + [VMEM] * (2 + len(others))
    if side == 0:
        return call(kernel, ins, [half] * 2, [late])(place, sent, early)
    scratch = [late] + [pltpu.VMEM(half, F32)] * 2 + [pltpu.SemaphoreType.DMA((4,))]
    return call(kernel, ins, [(NZ, CY, CX)] * 2, scratch, HBM)(place, sent, early, *others)


def body(head_start, class_map, class_cond, partials, send_count, recv_block):
    ngroups, ncols = lax.axis_size("rows"), lax.axis_size("cols")
    row = (CY, NZ, CX)
    scratch = [
        pltpu.SMEM((ncols,), jnp.int32),
        pltpu.VMEM((ncols, SLOTS, CX), F32),
        pltpu.VMEM((ncols, SLOTS + 8, CX), F32),
        pltpu.SemaphoreType.DMA,
        pltpu.SemaphoreType.DMA((4,)),
        pltpu.SemaphoreType.DMA((4,)),
    ]
    payload = call(outgoing_kernel, [HBM, HBM], [(ncols, SLOTS + 8, CX)], scratch, HBM)(
        in_hbm(send_count.reshape(ncols)), in_hbm(partials.reshape(ncols, SLOTS, CX))
    )[0]
    incoming = lax.all_to_all(payload, "cols", split_axis=0, concat_axis=0, tiled=True)
    flat = (NZ * CY, CX)
    scratch = [
        pltpu.SMEM((NCLASS,), F32),
        pltpu.VMEM(flat, F32),
        pltpu.VMEM(flat, jnp.int32),
        pltpu.VMEM((ncols, SLOTS), jnp.int32),
        pltpu.SemaphoreType.DMA((4,)),
    ]
    fields = (class_cond, head_start.reshape(flat), class_map.reshape(flat), recv_block.reshape(ncols, SLOTS))
    sizes = [row, row] + [(STRIP, 8, CX)] * 2 + [(EDGE, 8, CX)]
    head, cond, to_right, to_left, edge = call(fields_kernel, [HBM] * 4, sizes, scratch)(
        *(in_hbm(x) for x in fields)
    )
    left = lax.ppermute(to_right, "cols", forward(ncols))
    right = lax.ppermute(to_left, "cols", backward(ncols))
    edge = lax.ppermute(edge, "rows", backward(ngroups))
    main, halo, up, down = call(recharge_kernel, [VMEM] * 6 + [ANY], [row, row, (UP, 8, CX), (DOWN, 8, CX)])(
        incoming, to_right, left, right, head, cond, edge
    )
    top = lax.ppermute(down, "rows", forward(ngroups))
    bottom = lax.ppermute(up, "rows", backward(ngroups))
    place = jnp.stack([lax.axis_index("rows"), lax.axis_index("cols"), ngroups, ncols]).astype(jnp.int32)
    early = early_call(place, head, cond, main, halo, left, right)
    upper = late_call(0, place, top, early)
    return tuple(late_call(1, place, bottom, early, (edge, *upper)))


def solution(mesh):
    placed = (
        P(None, "rows", "cols"),
        P(None, "rows", "cols"),
        P(),
        P("rows", "cols", None, None, None),
        P("rows", "cols", None),
        P("rows", "cols", None, None),
    )
    return jax.shard_map(
        body,
        mesh=mesh,
        in_specs=placed,
        out_specs=(P(None, "rows", "cols"), P(None, "rows", "cols")),
        check_vma=False,
    )
```

```python
import functools

import jax
import jax.numpy as jnp
from jax import lax
from jax.experimental import pallas as pl
from jax.experimental.pallas import tpu as pltpu
from jax.sharding import PartitionSpec as P

NZ, CY, CX, SLOTS, NCLASS = 8, 32, 128, 32, 8
OMEGA = 0.8
NU1, NU2, NUC = 2, 2, 4
HY, HX = 14, 16
FY, RY = 13, 12
ROWS = CY + 2 * HY
LANES = 2 * CX
F32 = jnp.float32


def lane_of(shape):
    return lax.broadcasted_iota(jnp.int32, shape, len(shape) - 1)


def packed(rows, lane):
    out = None
    for q, row in enumerate(rows):
        turned = pltpu.roll(row, 32 * q + 16, 1)
        out = turned if q == 0 else jnp.where(lane // 32 == q, turned, out)
    return out


def unpacked(block, q, lane):
    turned = pltpu.roll(block, (CX - 32 * q - 16) % CX, 1)
    return jnp.where((lane < HX) | (lane >= CX - HX), turned, 0.0)


def outgoing_kernel(count_hbm, partials_hbm, class_cond_hbm, head_hbm, class_hbm, ids_hbm,
                    out_hbm, table_ref, head_ref, class_ref, ids_ref,
                    count_ref, class_cond_ref, partials_ref, out_ref, count_sem, in_sems, out_sems, field_sems):
    ncols = partials_ref.shape[0]
    part = ncols // 4
    counts = pltpu.make_async_copy(count_hbm, count_ref, count_sem)
    counts.start()
    arriving = []
    for c in range(4):
        piece = pl.ds(c * part, part)
        arriving.append(pltpu.make_async_copy(partials_hbm.at[piece], partials_ref.at[piece], in_sems.at[c]))
        arriving[c].start()
    pairs = (
        (class_cond_hbm, class_cond_ref), (head_hbm, head_ref), (class_hbm, class_ref), (ids_hbm, ids_ref)
    )
    fields = [pltpu.make_async_copy(a, b, field_sems.at[i]) for i, (a, b) in enumerate(pairs)]
    for copy in fields:
        copy.start()
    counts.wait()
    lane = lane_of((8, CX))
    slot = lax.broadcasted_iota(jnp.int32, (8, CX), 0)
    zero = jnp.zeros((8, CX), F32)
    strips, leaving, sent = [zero], [], 0
    for d in range(ncols):
        if d % part == 0:
            arriving[d // part].wait()
        rows = []
        for q in range(SLOTS // 8):
            row = jnp.where(slot + 8 * q < count_ref[d], partials_ref[d, 8 * q : 8 * q + 8, :], 0.0)
            out_ref[d, 8 * q : 8 * q + 8, :] = row
            rows.append(row)
        strips.append(packed(rows, lane))
        if d == ncols - 1:
            strips.append(zero)
        ready = d + 1 if d == ncols - 1 else d
        for i in range(max(0, d - 1), ready):
            out_ref[i, SLOTS : SLOTS + 8, :] = jnp.where(lane % 32 < HX, strips[i], strips[i + 2])
        if d % part == part - 1:
            piece = pl.ds(sent, ready - sent)
            leaving.append(pltpu.make_async_copy(out_ref.at[piece], out_hbm.at[piece], out_sems.at[d // part]))
            leaving[-1].start()
            sent = ready
    for copy in fields:
        copy.wait()
    for c in range(NCLASS):
        table_ref[c] = jnp.full((8, CX), class_cond_ref[c], F32)
    for copy in leaving:
        copy.wait()


def fields_kernel(table_ref, head_ref, class_ref, ids_ref, head_out, cond_out, right_out, left_out, edge_out):
    lane = lane_of((8, CX))
    values = [table_ref[c] for c in range(NCLASS)]
    blocks = []
    for block in range(CY // 4):
        heads, conds = [], []
        for q in range(4):
            y = 4 * block + q
            head = head_ref[pl.ds(y, NZ, stride=CY), :]
            kind = class_ref[pl.ds(y, NZ, stride=CY), :]
            cond = values[0]
            for c in range(1, NCLASS):
                cond = jnp.where(kind == c, values[c], cond)
            head_out[y] = head
            cond_out[y] = cond
            if y < FY:
                edge_out[y] = head
                edge_out[FY + y] = cond
            heads.append(head)
            conds.append(cond)
        blocks.append((packed(heads, lane), packed(conds, lane)))
    near = lane % 32 < HX
    for f in range(2):
        for i in range(CY // 8):
            one, two = blocks[2 * i][f], blocks[2 * i + 1][f]
            right_out[f * (CY // 8) + i] = jnp.where(near, one, pltpu.roll(two, HX, 1))
            left_out[f * (CY // 8) + i] = jnp.where(near, pltpu.roll(one, CX - HX, 1), two)
    ids = ids_ref[...].astype(F32)
    count = ids.shape[0] // 4
    for out in (right_out, left_out):
        out[STRIP - 1] = jnp.zeros((8, CX), F32)
        for r in range(count):
            row = jnp.concatenate([ids[4 * r + q : 4 * r + q + 1, :] for q in range(4)], axis=1)
            out[STRIP - 1, r : r + 1, :] = row


STRIP = CY // 4 + 1


def four_rows(left_ref, right_ref, f, i, lane):
    left, right = left_ref[f * (CY // 8) + i // 2], right_ref[f * (CY // 8) + i // 2]
    if i % 2 == 0:
        return jnp.where(lane % 32 < HX, left, pltpu.roll(right, HX, 1))
    return jnp.where(lane % 32 < HX, pltpu.roll(left, CX - HX, 1), right)


def recharge_kernel(incoming_ref, own_ref, left_ref, right_ref, head_ref, cond_ref, _,
                    main_out, halo_out, up_out, down_out):
    ncols = incoming_ref.shape[0]
    total = ncols * SLOTS
    chunk = min(256, total)
    senders = chunk // SLOTS
    lane = lane_of((8, CX))
    row = lax.broadcasted_iota(jnp.int32, (NZ * CY, chunk), 0)
    block_of = ((row % NZ) * CY + row // NZ).astype(F32)

    def onehot(ids, m):
        flat = jnp.concatenate([ids[r : r + 1, :] for r in range(m * chunk // CX, (m + 1) * chunk // CX)], axis=1)
        return jnp.where(block_of == flat, 1.0, 0.0).astype(jnp.bfloat16)

    def halves(values):
        high = values.astype(jnp.bfloat16)
        low = (values - high.astype(F32)).astype(jnp.bfloat16)
        return jnp.concatenate([high, low], axis=1)

    own, left, right = own_ref[STRIP - 1], left_ref[STRIP - 1], right_ref[STRIP - 1]
    main = jnp.zeros((NZ * CY, LANES), F32)
    from_left = jnp.zeros((NZ * CY, LANES), F32)
    from_right = jnp.zeros((NZ * CY, LANES), F32)
    for m in range(total // chunk):
        values = incoming_ref[m * senders : (m + 1) * senders, 0:SLOTS, :].reshape(chunk, CX)
        main = main + jnp.dot(onehot(own, m), halves(values), preferred_element_type=F32)
        strips = []
        for s in range(m * senders, (m + 1) * senders):
            strip = incoming_ref[s, SLOTS : SLOTS + 8, :]
            strips += [pltpu.roll(strip, (CX - 32 * q - 16) % CX, 1) for q in range(4)]
        edges = halves(jnp.concatenate(strips, axis=0))
        from_left = from_left + jnp.dot(onehot(left, m), edges, preferred_element_type=F32)
        from_right = from_right + jnp.dot(onehot(right, m), edges, preferred_element_type=F32)
    main = (main[:, :CX] + main[:, CX:]).reshape(CY, NZ, CX)
    from_left = (from_left[:, :CX] + from_left[:, CX:]).reshape(CY, NZ, CX)
    from_right = (from_right[:, :CX] + from_right[:, CX:]).reshape(CY, NZ, CX)
    wide = lane_of((CY, NZ, CX))
    halo = jnp.where(wide >= CX - HX, from_left, jnp.where(wide < HX, from_right, 0.0))
    main_out[...] = main
    halo_out[...] = halo
    for out, first, strip0, base in ((up_out, 0, 0, 0), (down_out, CY - HY, CY // 4 - 4, 2 * FY)):
        skip = first and HY - RY
        if base:
            out[0:FY] = head_ref[CY - FY : CY]
            out[FY : 2 * FY] = cond_ref[CY - FY : CY]
        out[base : base + RY] = main[first + skip : first + skip + RY]
        base = base + RY
        for i in range(4):
            for f in range(2):
                out[base + 4 * f + i] = four_rows(left_ref, right_ref, f, strip0 + i, lane)
        for i in range(RY // 4):
            y = first + skip + 4 * i
            out[base + 8 + i] = packed([halo[y + q] for q in range(4)], lane)


EDGE, UP = 2 * FY, RY + 8 + RY // 4
DOWN = EDGE + UP


def span(first, last):
    return list(range(first, last + 1))


NEEDED = {
    "u0": (span(1, 58), span(14, 45)),
    "half": (span(1, 58), span(14, 45)),
    "source": (span(2, 57), span(14, 45)),
    "fx": (span(2, 57), span(14, 45)),
    "fy": (span(1, 57), span(14, 44)),
    "fz": (span(2, 57), span(14, 45)),
    "weight": (span(2, 57), span(15, 44)),
    "u1": (span(2, 57), span(15, 44)),
    "u2": (span(3, 56), span(16, 43)),
    "c_half": (span(1, 28), span(7, 22)),
    "c_fx": (span(2, 27), span(7, 22)),
    "c_fy": (span(1, 27), span(7, 21)),
    "c_fz": (span(2, 27), span(7, 22)),
    "c_weight": (span(2, 27), span(8, 21)),
    "c_source": (span(2, 27), span(9, 20)),
    "c_u0": (span(2, 27), span(9, 20)),
    "c_u1": (span(3, 26), span(10, 19)),
    "c_u2": (span(4, 25), span(11, 18)),
    "c_u3": (span(5, 24), span(12, 17)),
    "u3": (span(11, 48), span(24, 35)),
    "u4": (span(12, 47), span(25, 34)),
    "u5": (span(13, 46), span(26, 33)),
    "residual": (span(14, 45), span(27, 32)),
}
EARLY, LATE = {}, ({}, {})
for _name, (_every, _own) in NEEDED.items():
    for _r in _every:
        _into = EARLY if _r in _own else LATE[0 if _r < _own[0] else 1]
        _into[_name, _r] = len(_into)


class Cycle:
    def __init__(self, place_ref, early, late=None, side=None):
        self.early, self.late, self.side = early, late, side
        self.lane = lane_of((1, NZ, LANES))
        layer = lax.broadcasted_iota(jnp.int32, (1, NZ, LANES), 1)
        self.below = jnp.where(layer < NZ - 1, 1.0, 0.0)
        self.even = self.lane % 2 == 0
        g, d, ngroups, ncols = place_ref[0], place_ref[1], place_ref[2], place_ref[3]
        right = jnp.where(d < ncols - 1, CX + HX, CX)
        left = jnp.where(d > 0, LANES - HX, LANES)
        columns = jnp.where((self.lane < right) | (self.lane >= left), OMEGA, 0.0)
        above, under = jnp.where(g > 0, 1.0, 0.0), jnp.where(g < ngroups - 1, 1.0, 0.0)
        self.inside = (columns * above, columns, columns * under)

    def ranges(self, name):
        every, own = NEEDED[name]
        if self.late is None:
            return [(own[0], len(own), 1)]
        if self.side == 0:
            return [(every[0], own[0] - every[0], 0)]
        return [(own[-1] + 1, every[-1] - own[-1], 2)]

    def get(self, name, r, n):
        parts, at = [], r
        while at < r + n:
            ref, rows = (self.early, EARLY) if (name, at) in EARLY else (self.late, LATE[self.side])
            many = 1
            while at + many < r + n and rows.get((name, at + many)) == rows[name, at] + many:
                many += 1
            parts.append(ref[pl.ds(rows[name, at], many)])
            at += many
        return parts[0] if len(parts) == 1 else jnp.concatenate(parts, axis=0)

    def put(self, name, r, n, value):
        if self.late is None:
            self.early[pl.ds(EARLY[name, r], n)] = value
        else:
            self.late[pl.ds(LATE[self.side][name, r], n)] = value

    def put_parts(self, name, r, main, halo):
        ref, at = (self.early, EARLY[name, r]) if self.late is None else (self.late, LATE[self.side][name, r])
        ref[at, :, 0:CX] = main
        ref[at, :, CX:LANES] = halo

    def turn(self, x, by):
        return pltpu.roll(x, by % LANES, 2)

    def turn_z(self, x, by):
        return pltpu.roll(x, by % NZ, 1)

    def pairs(self, x):
        two = x.reshape(x.shape[0] // 2, 2, NZ, LANES)
        two = two[:, 0] + two[:, 1]
        return two + jnp.where(self.even, self.turn(two, -1), self.turn(two, 1))

    def coefficients(self, mark, shift, zweight, own):
        for r, n, _ in self.ranges(mark + "fx"):
            k = self.get(mark + "half", r, n)
            self.put(mark + "fx", r, n, k + self.turn(k, -shift))
            self.put(mark + "fz", r, n, (k + self.turn_z(k, -1)) * (zweight * self.below))
        for r, n, _ in self.ranges(mark + "fy"):
            k = self.get(mark + "half", r, n + 1)
            self.put(mark + "fy", r, n, k[:-1] + k[1:])
        for r, n, part in self.ranges(mark + "weight"):
            pieces = [(r, n, part)]
            if part == 0:
                pieces = [(r, own[0] - r, 0), (own[0], r + n - own[0], 1)]
            elif part == 2:
                pieces = [(r, own[1] + 1 - r, 1), (own[1] + 1, r + n - own[1] - 1, 2)]
            for at, many, which in pieces:
                x, z = self.get(mark + "fx", at, many), self.get(mark + "fz", at, many)
                y = self.get(mark + "fy", at - 1, many + 1)
                total = (x + self.turn(x, shift)) + (y[1:] + y[:-1]) + (z + self.turn_z(z, 1))
                scale = self.inside[which]
                self.put(mark + "weight", at, many, scale / jnp.where(scale > 0.0, total, 1.0))

    def operator(self, u, mark, shift, r, n):
        v = self.get(u, r - 1, n + 2)
        own = v[1:-1]
        x = self.get(mark + "fx", r, n) * (own - self.turn(own, -shift))
        y = self.get(mark + "fy", r - 1, n + 1) * (v[:-1] - v[1:])
        z = self.get(mark + "fz", r, n) * (self.turn_z(own, -1) - own)
        return own, (x - self.turn(x, shift)) + (y[1:] - y[:-1]) + (z - self.turn_z(z, 1))

    def sweep(self, old, new, mark, shift):
        for r, n, _ in self.ranges(new):
            own, applied = self.operator(old, mark, shift, r, n)
            left = self.get(mark + "source", r, n) - applied
            self.put(new, r, n, own + self.get(mark + "weight", r, n) * left)

    def run(self, done):
        self.coefficients("", 1, 1.0, (HY, HY + CY - 1))
        self.sweep("u0", "u1", "", 1)
        self.sweep("u1", "u2", "", 1)
        for c, n, _ in self.ranges("c_half"):
            self.put("c_half", c, n, 0.25 * self.pairs(self.get("half", 2 * c, 2 * n)))
        self.coefficients("c_", 2, 4.0, (HY // 2, HY // 2 + CY // 2 - 1))
        for c, n, _ in self.ranges("c_source"):
            _, applied = self.operator("u2", "", 1, 2 * c, 2 * n)
            summed = self.pairs(self.get("source", 2 * c, 2 * n) - applied)
            self.put("c_source", c, n, summed)
            self.put("c_u0", c, n, self.get("c_weight", c, n) * summed)
        for i in range(1, NUC):
            self.sweep("c_u%d" % (i - 1), "c_u%d" % i, "c_", 2)
        for r, n, _ in self.ranges("u3"):
            c, many = r // 2, (r + n - 1) // 2 - r // 2 + 1
            added = self.get("c_u%d" % (NUC - 1), c, many)
            added = jnp.broadcast_to(added[:, None], (many, 2, NZ, LANES)).reshape(2 * many, NZ, LANES)
            self.put("u3", r, n, self.get("u2", r, n) + added[r % 2 : r % 2 + n])
        self.sweep("u3", "u4", "", 1)
        self.sweep("u4", "u5", "", 1)
        done()
        for r, n, _ in self.ranges("residual"):
            _, applied = self.operator("u5", "", 1, r, n)
            self.put("residual", r, n, self.get("source", r, n) - applied)


def early_kernel(place_ref, head_ref, cond_ref, main_ref, halo_ref, left_ref, right_ref, early):
    cycle = Cycle(place_ref, early)
    lane = lane_of((8, CX))
    for i in range(CY // 4):
        heads = four_rows(left_ref, right_ref, 0, i, lane)
        conds = 0.5 * four_rows(left_ref, right_ref, 1, i, lane)
        for q in range(4):
            y = 4 * i + q
            cycle.put_parts("u0", HY + y, head_ref[y], unpacked(heads, q, lane))
            cycle.put_parts("half", HY + y, 0.5 * cond_ref[y], unpacked(conds, q, lane))
            cycle.put_parts("source", HY + y, main_ref[y], halo_ref[y])
    cycle.run(lambda: None)


def late_kernel(side, place_ref, sent_ref, early, *refs):
    copies = []
    if side == 0:
        head_ref, residual_ref, late = refs
        edge_ref = sent_ref
    else:
        edge_ref, upper_head, upper_residual, head_hbm, residual_hbm, late, head_ref, residual_ref, sems = refs
        top, bottom = pl.ds(0, CY // 2), pl.ds(CY // 2, CY // 2)
        pairs = (
            (upper_head, head_hbm.at[:, top, :]), (upper_residual, residual_hbm.at[:, top, :]),
            (head_ref, head_hbm.at[:, bottom, :]), (residual_ref, residual_hbm.at[:, bottom, :]),
        )
        copies = [pltpu.make_async_copy(a, b, sems.at[i]) for i, (a, b) in enumerate(pairs)]
        copies[0].start()
        copies[1].start()
    cycle = Cycle(place_ref, early, late, side)
    lane = lane_of((8, CX))
    base, source = (EDGE + RY, EDGE) if side == 0 else (RY, 0)
    first, shift, skip = ((0, 2, HY - RY), (HY + CY, 0, 0))[side]
    for row in range(FY):
        i = row + HY - FY if side == 0 else row
        at, q = (i + shift) // 4, (i + shift) % 4
        cycle.put_parts("u0", first + i, edge_ref[row], unpacked(sent_ref[base + at], q, lane))
        half = 0.5 * edge_ref[FY + row]
        cycle.put_parts("half", first + i, half, 0.5 * unpacked(sent_ref[base + 4 + at], q, lane))
    for i in range(RY):
        edge = unpacked(sent_ref[base + 8 + i // 4], i % 4, lane)
        cycle.put_parts("source", first + skip + i, sent_ref[source + i], edge)

    def leave(name, ref):
        for y in range(CY // 2):
            ref[:, y, :] = cycle.get(name, HY + side * (CY // 2) + y, 1)[0, :, 0:CX]

    def head_done():
        leave("u5", head_ref)
        for copy in copies[2:3]:
            copy.start()

    cycle.run(head_done)
    leave("residual", residual_ref)
    for copy in copies[3:]:
        copy.start()
    for copy in copies:
        copy.wait()


VMEM = pl.BlockSpec(memory_space=pltpu.VMEM)
SMEM = pl.BlockSpec(memory_space=pltpu.SMEM)
HBM = pl.BlockSpec(memory_space=pltpu.HBM)
ANY = pl.BlockSpec(memory_space=pl.ANY)


def in_hbm(x):
    return pltpu.with_memory_space_constraint(x, pltpu.HBM)


def call(kernel, ins, outs, scratch=(), out=VMEM, flops=1 << 20, nbytes=1 << 20):
    return pl.pallas_call(
        kernel,
        out_shape=tuple(jax.ShapeDtypeStruct(*s) if isinstance(s[0], tuple) else jax.ShapeDtypeStruct(s, F32) for s in outs),
        in_specs=ins,
        out_specs=out if isinstance(out, tuple) else (out,) * len(outs),
        scratch_shapes=scratch,
        cost_estimate=pl.CostEstimate(flops=flops, bytes_accessed=nbytes, transcendentals=0),
        compiler_params=pltpu.CompilerParams(vmem_limit_bytes=32 << 20),
    )


def forward(count):
    return [(i, i + 1) for i in range(count - 1)]


def backward(count):
    return [(i + 1, i) for i in range(count - 1)]


def early_call(place, head, cond, main, halo, left, right):
    return call(early_kernel, [SMEM] + [VMEM] * 6, [(len(EARLY), NZ, LANES)])(
        place, head, cond, main, halo, left, right
    )[0]


def late_call(side, place, sent, early, others=()):
    half = (NZ, CY // 2, CX)
    late = pltpu.VMEM((len(LATE[side]), NZ, LANES), F32)
    kernel, ins = functools.partial(late_kernel, side), [SMEM] + [VMEM] * (2 + len(others))
    if side == 0:
        return call(kernel, ins, [half] * 2, [late])(place, sent, early)
    scratch = [late] + [pltpu.VMEM(half, F32)] * 2 + [pltpu.SemaphoreType.DMA((4,))]
    return call(kernel, ins, [(NZ, CY, CX)] * 2, scratch, HBM)(place, sent, early, *others)


def body(head_start, class_map, class_cond, partials, send_count, recv_block):
    ngroups, ncols = lax.axis_size("rows"), lax.axis_size("cols")
    row = (CY, NZ, CX)
    flat = (NZ * CY, CX)
    scratch = [
        pltpu.SMEM((ncols,), jnp.int32),
        pltpu.SMEM((NCLASS,), F32),
        pltpu.VMEM((ncols, SLOTS, CX), F32),
        pltpu.VMEM((ncols, SLOTS + 8, CX), F32),
        pltpu.SemaphoreType.DMA,
        pltpu.SemaphoreType.DMA((4,)),
        pltpu.SemaphoreType.DMA((4,)),
        pltpu.SemaphoreType.DMA((4,)),
    ]
    ids = (ncols, SLOTS)
    given = (
        send_count.reshape(ncols), partials.reshape(ncols, SLOTS, CX),
        class_cond, head_start.reshape(flat), class_map.reshape(flat), recv_block.reshape(ids),
    )
    sizes = [(ncols, SLOTS + 8, CX), (NCLASS, 8, CX), flat, (flat, jnp.int32), (ids, jnp.int32)]
    payload, *fields = call(outgoing_kernel, [HBM] * 6, sizes, scratch, (HBM,) + (VMEM,) * 4)(*map(in_hbm, given))
    incoming = lax.all_to_all(payload, "cols", split_axis=0, concat_axis=0, tiled=True)
    sizes = [row, row] + [(STRIP, 8, CX)] * 2 + [(EDGE, 8, CX)]
    head, cond, to_right, to_left, edge = call(fields_kernel, [VMEM] * 4, sizes)(*fields)
    left = lax.ppermute(to_right, "cols", forward(ncols))
    right = lax.ppermute(to_left, "cols", backward(ncols))
    edge = lax.ppermute(edge, "rows", backward(ngroups))
    main, halo, up, down = call(recharge_kernel, [VMEM] * 6 + [ANY], [row, row, (UP, 8, CX), (DOWN, 8, CX)])(
        incoming, to_right, left, right, head, cond, edge
    )
    top = lax.ppermute(down, "rows", forward(ngroups))
    bottom = lax.ppermute(up, "rows", backward(ngroups))
    place = jnp.stack([lax.axis_index("rows"), lax.axis_index("cols"), ngroups, ncols]).astype(jnp.int32)
    early = early_call(place, head, cond, main, halo, left, right)
    upper = late_call(0, place, top, early)
    return tuple(late_call(1, place, bottom, early, (edge, *upper)))


def solution(mesh):
    placed = (
        P(None, "rows", "cols"),
        P(None, "rows", "cols"),
        P(),
        P("rows", "cols", None, None, None),
        P("rows", "cols", None),
        P("rows", "cols", None, None),
    )
    return jax.shard_map(
        body,
        mesh=mesh,
        in_specs=placed,
        out_specs=(P(None, "rows", "cols"), P(None, "rows", "cols")),
        check_vma=False,
    )
```

```python
import functools

import jax
import jax.numpy as jnp
from jax import lax
from jax.experimental import pallas as pl
from jax.experimental.pallas import tpu as pltpu
from jax.sharding import PartitionSpec as P

NZ, CY, CX, SLOTS, NCLASS = 8, 32, 128, 32, 8
OMEGA = 0.8
NU1, NU2, NUC = 2, 2, 4
HY, HX = 14, 16
FY, RY = 13, 12
ROWS = CY + 2 * HY
LANES = 2 * CX
F32 = jnp.float32


def lane_of(shape):
    return lax.broadcasted_iota(jnp.int32, shape, len(shape) - 1)


def packed(rows, lane):
    out = None
    for q, row in enumerate(rows):
        turned = pltpu.roll(row, 32 * q + 16, 1)
        out = turned if q == 0 else jnp.where(lane // 32 == q, turned, out)
    return out


def unpacked(block, q, lane):
    turned = pltpu.roll(block, (CX - 32 * q - 16) % CX, 1)
    return jnp.where((lane < HX) | (lane >= CX - HX), turned, 0.0)


def outgoing_kernel(count_hbm, partials_hbm, class_cond_hbm, head_hbm, class_hbm, ids_hbm,
                    out_hbm, table_ref, head_ref, class_ref, ids_ref,
                    count_ref, class_cond_ref, partials_ref, out_ref, count_sem, in_sems, out_sems, field_sems):
    ncols = partials_ref.shape[0]
    part = max(ncols // 8, 1)
    pieces = ncols // part
    counts = pltpu.make_async_copy(count_hbm, count_ref, count_sem)
    counts.start()
    arriving = []
    for c in range(pieces):
        piece = pl.ds(c * part, part)
        arriving.append(pltpu.make_async_copy(partials_hbm.at[piece], partials_ref.at[piece], in_sems.at[c]))
        arriving[c].start()
    pairs = (
        (class_cond_hbm, class_cond_ref), (head_hbm, head_ref), (class_hbm, class_ref), (ids_hbm, ids_ref)
    )
    fields = [pltpu.make_async_copy(a, b, field_sems.at[i]) for i, (a, b) in enumerate(pairs)]
    for copy in fields:
        copy.start()
    counts.wait()
    lane = lane_of((8, CX))
    slot = lax.broadcasted_iota(jnp.int32, (8, CX), 0)
    zero = jnp.zeros((8, CX), F32)
    strips, leaving, sent = [zero], [], 0
    for d in range(ncols):
        if d % part == 0:
            arriving[d // part].wait()
        rows = []
        for q in range(SLOTS // 8):
            row = jnp.where(slot + 8 * q < count_ref[d], partials_ref[d, 8 * q : 8 * q + 8, :], 0.0)
            out_ref[d, 8 * q : 8 * q + 8, :] = row
            rows.append(row)
        strips.append(packed(rows, lane))
        if d == ncols - 1:
            strips.append(zero)
        ready = d + 1 if d == ncols - 1 else d
        for i in range(max(0, d - 1), ready):
            out_ref[i, SLOTS : SLOTS + 8, :] = jnp.where(lane % 32 < HX, strips[i], strips[i + 2])
        if d % part == part - 1:
            piece = pl.ds(sent, ready - sent)
            leaving.append(pltpu.make_async_copy(out_ref.at[piece], out_hbm.at[piece], out_sems.at[d // part]))
            leaving[-1].start()
            sent = ready
    for copy in fields:
        copy.wait()
    for c in range(NCLASS):
        table_ref[c] = jnp.full((8, CX), class_cond_ref[c], F32)
    for copy in leaving:
        copy.wait()


def fields_kernel(table_ref, head_ref, class_ref, ids_ref, head_out, cond_out, right_out, left_out, edge_out):
    lane = lane_of((8, CX))
    values = [table_ref[c] for c in range(NCLASS)]
    blocks = []
    for block in range(CY // 4):
        heads, conds = [], []
        for q in range(4):
            y = 4 * block + q
            head = head_ref[pl.ds(y, NZ, stride=CY), :]
            kind = class_ref[pl.ds(y, NZ, stride=CY), :]
            cond = values[0]
            for c in range(1, NCLASS):
                cond = jnp.where(kind == c, values[c], cond)
            head_out[y] = head
            cond_out[y] = cond
            if y < FY:
                edge_out[y] = head
                edge_out[FY + y] = cond
            heads.append(head)
            conds.append(cond)
        blocks.append((packed(heads, lane), packed(conds, lane)))
    near = lane % 32 < HX
    for f in range(2):
        for i in range(CY // 8):
            one, two = blocks[2 * i][f], blocks[2 * i + 1][f]
            right_out[f * (CY // 8) + i] = jnp.where(near, one, pltpu.roll(two, HX, 1))
            left_out[f * (CY // 8) + i] = jnp.where(near, pltpu.roll(one, CX - HX, 1), two)
    ids = ids_ref[...].astype(F32)
    count = ids.shape[0] // 4
    for out in (right_out, left_out):
        out[STRIP - 1] = jnp.zeros((8, CX), F32)
        for r in range(count):
            row = jnp.concatenate([ids[4 * r + q : 4 * r + q + 1, :] for q in range(4)], axis=1)
            out[STRIP - 1, r : r + 1, :] = row


STRIP = CY // 4 + 1


def four_rows(left_ref, right_ref, f, i, lane):
    left, right = left_ref[f * (CY // 8) + i // 2], right_ref[f * (CY // 8) + i // 2]
    if i % 2 == 0:
        return jnp.where(lane % 32 < HX, left, pltpu.roll(right, HX, 1))
    return jnp.where(lane % 32 < HX, pltpu.roll(left, CX - HX, 1), right)


def recharge_kernel(incoming_ref, own_ref, left_ref, right_ref, head_ref, cond_ref, _,
                    main_out, halo_out, up_out, down_out):
    ncols = incoming_ref.shape[0]
    total = ncols * SLOTS
    chunk = min(256, total)
    senders = chunk // SLOTS
    lane = lane_of((8, CX))
    row = lax.broadcasted_iota(jnp.int32, (NZ * CY, chunk), 0)
    block_of = ((row % NZ) * CY + row // NZ).astype(F32)

    def onehot(ids, m):
        flat = jnp.concatenate([ids[r : r + 1, :] for r in range(m * chunk // CX, (m + 1) * chunk // CX)], axis=1)
        return jnp.where(block_of == flat, 1.0, 0.0).astype(jnp.bfloat16)

    def halves(values):
        high = values.astype(jnp.bfloat16)
        low = (values - high.astype(F32)).astype(jnp.bfloat16)
        return jnp.concatenate([high, low], axis=1)

    own, left, right = own_ref[STRIP - 1], left_ref[STRIP - 1], right_ref[STRIP - 1]
    main = jnp.zeros((NZ * CY, LANES), F32)
    from_left = jnp.zeros((NZ * CY, LANES), F32)
    from_right = jnp.zeros((NZ * CY, LANES), F32)
    for m in range(total // chunk):
        values = incoming_ref[m * senders : (m + 1) * senders, 0:SLOTS, :].reshape(chunk, CX)
        main = main + jnp.dot(onehot(own, m), halves(values), preferred_element_type=F32)
        strips = []
        for s in range(m * senders, (m + 1) * senders):
            strip = incoming_ref[s, SLOTS : SLOTS + 8, :]
            strips += [pltpu.roll(strip, (CX - 32 * q - 16) % CX, 1) for q in range(4)]
        edges = halves(jnp.concatenate(strips, axis=0))
        from_left = from_left + jnp.dot(onehot(left, m), edges, preferred_element_type=F32)
        from_right = from_right + jnp.dot(onehot(right, m), edges, preferred_element_type=F32)
    main = (main[:, :CX] + main[:, CX:]).reshape(CY, NZ, CX)
    from_left = (from_left[:, :CX] + from_left[:, CX:]).reshape(CY, NZ, CX)
    from_right = (from_right[:, :CX] + from_right[:, CX:]).reshape(CY, NZ, CX)
    wide = lane_of((CY, NZ, CX))
    halo = jnp.where(wide >= CX - HX, from_left, jnp.where(wide < HX, from_right, 0.0))
    main_out[...] = main
    halo_out[...] = halo
    for out, first, strip0, base in ((up_out, 0, 0, 0), (down_out, CY - HY, CY // 4 - 4, 2 * FY)):
        skip = first and HY - RY
        if base:
            out[0:FY] = head_ref[CY - FY : CY]
            out[FY : 2 * FY] = cond_ref[CY - FY : CY]
        out[base : base + RY] = main[first + skip : first + skip + RY]
        base = base + RY
        for i in range(4):
            for f in range(2):
                out[base + 4 * f + i] = four_rows(left_ref, right_ref, f, strip0 + i, lane)
        for i in range(RY // 4):
            y = first + skip + 4 * i
            out[base + 8 + i] = packed([halo[y + q] for q in range(4)], lane)


EDGE, UP = 2 * FY, RY + 8 + RY // 4
DOWN = EDGE + UP


def span(first, last):
    return list(range(first, last + 1))


NEEDED = {
    "u0": (span(1, 58), span(14, 45)),
    "half": (span(1, 58), span(14, 45)),
    "source": (span(2, 57), span(14, 45)),
    "fx": (span(2, 57), span(14, 45)),
    "fy": (span(1, 57), span(14, 44)),
    "fz": (span(2, 57), span(14, 45)),
    "weight": (span(2, 57), span(15, 44)),
    "u1": (span(2, 57), span(15, 44)),
    "u2": (span(3, 56), span(16, 43)),
    "c_half": (span(1, 28), span(7, 22)),
    "c_fx": (span(2, 27), span(7, 22)),
    "c_fy": (span(1, 27), span(7, 21)),
    "c_fz": (span(2, 27), span(7, 22)),
    "c_weight": (span(2, 27), span(8, 21)),
    "c_source": (span(2, 27), span(9, 20)),
    "c_u0": (span(2, 27), span(9, 20)),
    "c_u1": (span(3, 26), span(10, 19)),
    "c_u2": (span(4, 25), span(11, 18)),
    "c_u3": (span(5, 24), span(12, 17)),
    "u3": (span(11, 48), span(24, 35)),
    "u4": (span(12, 47), span(25, 34)),
    "u5": (span(13, 46), span(26, 33)),
    "residual": (span(14, 45), span(27, 32)),
}
EARLY, LATE = {}, ({}, {})
for _name, (_every, _own) in NEEDED.items():
    for _r in _every:
        _into = EARLY if _r in _own else LATE[0 if _r < _own[0] else 1]
        _into[_name, _r] = len(_into)


class Cycle:
    def __init__(self, place_ref, early, late=None, side=None):
        self.early, self.late, self.side = early, late, side
        self.lane = lane_of((1, NZ, LANES))
        layer = lax.broadcasted_iota(jnp.int32, (1, NZ, LANES), 1)
        self.below = jnp.where(layer < NZ - 1, 1.0, 0.0)
        self.even = self.lane % 2 == 0
        g, d, ngroups, ncols = place_ref[0], place_ref[1], place_ref[2], place_ref[3]
        right = jnp.where(d < ncols - 1, CX + HX, CX)
        left = jnp.where(d > 0, LANES - HX, LANES)
        columns = jnp.where((self.lane < right) | (self.lane >= left), OMEGA, 0.0)
        above, under = jnp.where(g > 0, 1.0, 0.0), jnp.where(g < ngroups - 1, 1.0, 0.0)
        self.inside = (columns * above, columns, columns * under)

    def ranges(self, name):
        every, own = NEEDED[name]
        if self.late is None:
            return [(own[0], len(own), 1)]
        if self.side == 0:
            return [(every[0], own[0] - every[0], 0)]
        return [(own[-1] + 1, every[-1] - own[-1], 2)]

    def get(self, name, r, n):
        parts, at = [], r
        while at < r + n:
            ref, rows = (self.early, EARLY) if (name, at) in EARLY else (self.late, LATE[self.side])
            many = 1
            while at + many < r + n and rows.get((name, at + many)) == rows[name, at] + many:
                many += 1
            parts.append(ref[pl.ds(rows[name, at], many)])
            at += many
        return parts[0] if len(parts) == 1 else jnp.concatenate(parts, axis=0)

    def put(self, name, r, n, value):
        if self.late is None:
            self.early[pl.ds(EARLY[name, r], n)] = value
        else:
            self.late[pl.ds(LATE[self.side][name, r], n)] = value

    def put_parts(self, name, r, main, halo):
        ref, at = (self.early, EARLY[name, r]) if self.late is None else (self.late, LATE[self.side][name, r])
        ref[at, :, 0:CX] = main
        ref[at, :, CX:LANES] = halo

    def turn(self, x, by):
        return pltpu.roll(x, by % LANES, 2)

    def turn_z(self, x, by):
        return pltpu.roll(x, by % NZ, 1)

    def pairs(self, x):
        two = x.reshape(x.shape[0] // 2, 2, NZ, LANES)
        two = two[:, 0] + two[:, 1]
        return two + jnp.where(self.even, self.turn(two, -1), self.turn(two, 1))

    def coefficients(self, mark, shift, zweight, own):
        for r, n, _ in self.ranges(mark + "fx"):
            k = self.get(mark + "half", r, n)
            self.put(mark + "fx", r, n, k + self.turn(k, -shift))
            self.put(mark + "fz", r, n, (k + self.turn_z(k, -1)) * (zweight * self.below))
        for r, n, _ in self.ranges(mark + "fy"):
            k = self.get(mark + "half", r, n + 1)
            self.put(mark + "fy", r, n, k[:-1] + k[1:])
        for r, n, part in self.ranges(mark + "weight"):
            pieces = [(r, n, part)]
            if part == 0:
                pieces = [(r, own[0] - r, 0), (own[0], r + n - own[0], 1)]
            elif part == 2:
                pieces = [(r, own[1] + 1 - r, 1), (own[1] + 1, r + n - own[1] - 1, 2)]
            for at, many, which in pieces:
                x, z = self.get(mark + "fx", at, many), self.get(mark + "fz", at, many)
                y = self.get(mark + "fy", at - 1, many + 1)
                total = (x + self.turn(x, shift)) + (y[1:] + y[:-1]) + (z + self.turn_z(z, 1))
                scale = self.inside[which]
                self.put(mark + "weight", at, many, scale / jnp.where(scale > 0.0, total, 1.0))

    def operator(self, u, mark, shift, r, n):
        v = self.get(u, r - 1, n + 2)
        own = v[1:-1]
        x = self.get(mark + "fx", r, n) * (own - self.turn(own, -shift))
        y = self.get(mark + "fy", r - 1, n + 1) * (v[:-1] - v[1:])
        z = self.get(mark + "fz", r, n) * (self.turn_z(own, -1) - own)
        return own, (x - self.turn(x, shift)) + (y[1:] - y[:-1]) + (z - self.turn_z(z, 1))

    def sweep(self, old, new, mark, shift):
        for r, n, _ in self.ranges(new):
            own, applied = self.operator(old, mark, shift, r, n)
            left = self.get(mark + "source", r, n) - applied
            self.put(new, r, n, own + self.get(mark + "weight", r, n) * left)

    def run(self, done):
        self.coefficients("", 1, 1.0, (HY, HY + CY - 1))
        self.sweep("u0", "u1", "", 1)
        self.sweep("u1", "u2", "", 1)
        for c, n, _ in self.ranges("c_half"):
            self.put("c_half", c, n, 0.25 * self.pairs(self.get("half", 2 * c, 2 * n)))
        self.coefficients("c_", 2, 4.0, (HY // 2, HY // 2 + CY // 2 - 1))
        for c, n, _ in self.ranges("c_source"):
            _, applied = self.operator("u2", "", 1, 2 * c, 2 * n)
            summed = self.pairs(self.get("source", 2 * c, 2 * n) - applied)
            self.put("c_source", c, n, summed)
            self.put("c_u0", c, n, self.get("c_weight", c, n) * summed)
        for i in range(1, NUC):
            self.sweep("c_u%d" % (i - 1), "c_u%d" % i, "c_", 2)
        for r, n, _ in self.ranges("u3"):
            c, many = r // 2, (r + n - 1) // 2 - r // 2 + 1
            added = self.get("c_u%d" % (NUC - 1), c, many)
            added = jnp.broadcast_to(added[:, None], (many, 2, NZ, LANES)).reshape(2 * many, NZ, LANES)
            self.put("u3", r, n, self.get("u2", r, n) + added[r % 2 : r % 2 + n])
        self.sweep("u3", "u4", "", 1)
        self.sweep("u4", "u5", "", 1)
        done()
        for r, n, _ in self.ranges("residual"):
            _, applied = self.operator("u5", "", 1, r, n)
            self.put("residual", r, n, self.get("source", r, n) - applied)


def early_kernel(place_ref, head_ref, cond_ref, main_ref, halo_ref, left_ref, right_ref, early):
    cycle = Cycle(place_ref, early)
    lane = lane_of((8, CX))
    for i in range(CY // 4):
        heads = four_rows(left_ref, right_ref, 0, i, lane)
        conds = 0.5 * four_rows(left_ref, right_ref, 1, i, lane)
        for q in range(4):
            y = 4 * i + q
            cycle.put_parts("u0", HY + y, head_ref[y], unpacked(heads, q, lane))
            cycle.put_parts("half", HY + y, 0.5 * cond_ref[y], unpacked(conds, q, lane))
            cycle.put_parts("source", HY + y, main_ref[y], halo_ref[y])
    cycle.run(lambda: None)


def late_kernel(side, place_ref, sent_ref, early, *refs):
    copies = []
    if side == 0:
        head_ref, residual_ref, late = refs
        edge_ref = sent_ref
    else:
        edge_ref, upper_head, upper_residual, head_hbm, residual_hbm, late, head_ref, residual_ref, sems = refs
        top, bottom = pl.ds(0, CY // 2), pl.ds(CY // 2, CY // 2)
        pairs = (
            (upper_head, head_hbm.at[:, top, :]), (upper_residual, residual_hbm.at[:, top, :]),
            (head_ref, head_hbm.at[:, bottom, :]), (residual_ref, residual_hbm.at[:, bottom, :]),
        )
        copies = [pltpu.make_async_copy(a, b, sems.at[i]) for i, (a, b) in enumerate(pairs)]
        copies[0].start()
        copies[1].start()
    cycle = Cycle(place_ref, early, late, side)
    lane = lane_of((8, CX))
    base, source = (EDGE + RY, EDGE) if side == 0 else (RY, 0)
    first, shift, skip = ((0, 2, HY - RY), (HY + CY, 0, 0))[side]
    for row in range(FY):
        i = row + HY - FY if side == 0 else row
        at, q = (i + shift) // 4, (i + shift) % 4
        cycle.put_parts("u0", first + i, edge_ref[row], unpacked(sent_ref[base + at], q, lane))
        half = 0.5 * edge_ref[FY + row]
        cycle.put_parts("half", first + i, half, 0.5 * unpacked(sent_ref[base + 4 + at], q, lane))
    for i in range(RY):
        edge = unpacked(sent_ref[base + 8 + i // 4], i % 4, lane)
        cycle.put_parts("source", first + skip + i, sent_ref[source + i], edge)

    def leave(name, ref):
        for y in range(CY // 2):
            ref[:, y, :] = cycle.get(name, HY + side * (CY // 2) + y, 1)[0, :, 0:CX]

    def head_done():
        leave("u5", head_ref)
        for copy in copies[2:3]:
            copy.start()

    cycle.run(head_done)
    leave("residual", residual_ref)
    for copy in copies[3:]:
        copy.start()
    for copy in copies:
        copy.wait()


VMEM = pl.BlockSpec(memory_space=pltpu.VMEM)
SMEM = pl.BlockSpec(memory_space=pltpu.SMEM)
HBM = pl.BlockSpec(memory_space=pltpu.HBM)
ANY = pl.BlockSpec(memory_space=pl.ANY)


def in_hbm(x):
    return pltpu.with_memory_space_constraint(x, pltpu.HBM)


def call(kernel, ins, outs, scratch=(), out=VMEM, flops=1 << 20, nbytes=1 << 20):
    return pl.pallas_call(
        kernel,
        out_shape=tuple(jax.ShapeDtypeStruct(*s) if isinstance(s[0], tuple) else jax.ShapeDtypeStruct(s, F32) for s in outs),
        in_specs=ins,
        out_specs=out if isinstance(out, tuple) else (out,) * len(outs),
        scratch_shapes=scratch,
        cost_estimate=pl.CostEstimate(flops=flops, bytes_accessed=nbytes, transcendentals=0),
        compiler_params=pltpu.CompilerParams(vmem_limit_bytes=32 << 20),
    )


def forward(count):
    return [(i, i + 1) for i in range(count - 1)]


def backward(count):
    return [(i + 1, i) for i in range(count - 1)]


def early_call(place, head, cond, main, halo, left, right):
    return call(early_kernel, [SMEM] + [VMEM] * 6, [(len(EARLY), NZ, LANES)])(
        place, head, cond, main, halo, left, right
    )[0]


def late_call(side, place, sent, early, others=()):
    half = (NZ, CY // 2, CX)
    late = pltpu.VMEM((len(LATE[side]), NZ, LANES), F32)
    kernel, ins = functools.partial(late_kernel, side), [SMEM] + [VMEM] * (2 + len(others))
    if side == 0:
        return call(kernel, ins, [half] * 2, [late])(place, sent, early)
    scratch = [late] + [pltpu.VMEM(half, F32)] * 2 + [pltpu.SemaphoreType.DMA((4,))]
    return call(kernel, ins, [(NZ, CY, CX)] * 2, scratch, HBM)(place, sent, early, *others)


def body(head_start, class_map, class_cond, partials, send_count, recv_block):
    ngroups, ncols = lax.axis_size("rows"), lax.axis_size("cols")
    row = (CY, NZ, CX)
    flat = (NZ * CY, CX)
    scratch = [
        pltpu.SMEM((ncols,), jnp.int32),
        pltpu.SMEM((NCLASS,), F32),
        pltpu.VMEM((ncols, SLOTS, CX), F32),
        pltpu.VMEM((ncols, SLOTS + 8, CX), F32),
        pltpu.SemaphoreType.DMA,
        pltpu.SemaphoreType.DMA((8,)),
        pltpu.SemaphoreType.DMA((8,)),
        pltpu.SemaphoreType.DMA((4,)),
    ]
    ids = (ncols, SLOTS)
    given = (
        send_count.reshape(ncols), partials.reshape(ncols, SLOTS, CX),
        class_cond, head_start.reshape(flat), class_map.reshape(flat), recv_block.reshape(ids),
    )
    sizes = [(ncols, SLOTS + 8, CX), (NCLASS, 8, CX), flat, (flat, jnp.int32), (ids, jnp.int32)]
    payload, *fields = call(outgoing_kernel, [HBM] * 6, sizes, scratch, (HBM,) + (VMEM,) * 4)(*map(in_hbm, given))
    incoming = lax.all_to_all(payload, "cols", split_axis=0, concat_axis=0, tiled=True)
    sizes = [row, row] + [(STRIP, 8, CX)] * 2 + [(EDGE, 8, CX)]
    head, cond, to_right, to_left, edge = call(fields_kernel, [VMEM] * 4, sizes)(*fields)
    left = lax.ppermute(to_right, "cols", forward(ncols))
    right = lax.ppermute(to_left, "cols", backward(ncols))
    edge = lax.ppermute(edge, "rows", backward(ngroups))
    main, halo, up, down = call(recharge_kernel, [VMEM] * 6 + [ANY], [row, row, (UP, 8, CX), (DOWN, 8, CX)])(
        incoming, to_right, left, right, head, cond, edge
    )
    top = lax.ppermute(down, "rows", forward(ngroups))
    bottom = lax.ppermute(up, "rows", backward(ngroups))
    place = jnp.stack([lax.axis_index("rows"), lax.axis_index("cols"), ngroups, ncols]).astype(jnp.int32)
    early = early_call(place, head, cond, main, halo, left, right)
    upper = late_call(0, place, top, early)
    return tuple(late_call(1, place, bottom, early, (edge, *upper)))


def solution(mesh):
    placed = (
        P(None, "rows", "cols"),
        P(None, "rows", "cols"),
        P(),
        P("rows", "cols", None, None, None),
        P("rows", "cols", None),
        P("rows", "cols", None, None),
    )
    return jax.shard_map(
        body,
        mesh=mesh,
        in_specs=placed,
        out_specs=(P(None, "rows", "cols"), P(None, "rows", "cols")),
        check_vma=False,
    )
```
